256 devices in a mesh: dp: 16 (over x, y), expert: 16 (over z, core).
Axes of the slice: x: 4, y: 4, z: 8, core: 2. Of those that a mesh axis runs over, the one named last changes fastest.
Arguments:
- tokens: bfloat16 [40960, 2048], P(('dp', 'expert')), may hold values from -6 to 6
- routes: int32 [40960, 2], P(('dp', 'expert')), may hold values from 0 to 15, all different within a row; in each aligned block of 160 rows (0 to 159, 160 to 319, ...) at most 30 rows name the same one
- route_gains: float32 [40960, 2], P(('dp', 'expert')), may hold values from 0.1 to 1
- cotangent: bfloat16 [40960, 2048], P(('dp', 'expert')), may hold values from -24 to 24
- w_gate: bfloat16 [16, 2048, 768], P('expert'), may hold values from -0.125 to 0.125
- w_up: bfloat16 [16, 2048, 768], P('expert'), may hold values from -0.125 to 0.125
- w_down: bfloat16 [16, 2048, 768], P('expert'), may hold values from -0.21875 to 0.21875
Outputs:
- layer_output: bfloat16 [40960, 2048], P(('dp', 'expert'))
- input_grad: bfloat16 [40960, 2048], P(('dp', 'expert'))
- grad_gate: bfloat16 [16, 2048, 768], P('expert', 'dp')
- grad_up: bfloat16 [16, 2048, 768], P('expert', 'dp')
- grad_down: bfloat16 [16, 2048, 768], P('expert', 'dp')
The draws below stay inside these ranges and needn't reach their ends.
Inputs may be any that keep to these rules, and one draw needn't show every extreme that they name: `routes`: each row names 2 different experts. Within the rows of one device (aligned blocks of 160 rows) no expert is named more than 30 times, and in some device's rows one expert is named exactly 30 times.
All inputs are finite; a program needn't handle non-finite values.
Results may differ from the reference program's by a relative error of at most 0.015.
Values may be sent and summed in bfloat16 or wider, within the bound.
A program may use at most 128 MiB of HBM per device.

```python
import math
import jax
import jax.numpy as jnp
import numpy as np
from jax import lax

D = 2048
FF = 768
TOP = 2
TOK_DEV = 160
EXPERTS = 16
CAP = 30
TOKENS = 40960
N_DP = 16
N_EXPERT = 16


def strengthened(drawn, stream_key, source, target, blocks, factor):
    owner, partner = [(jnp.arange(drawn.shape[dim]) // (drawn.shape[dim] // blocks)).reshape([-1 if axis == dim else 1 for axis in range(drawn.ndim)]) for dim in (source, target)]
    chosen = jax.random.permutation(stream_key, blocks)[partner]
    strong = (owner == chosen) | (owner == (partner + blocks // 2) % blocks)
    return jnp.where(strong, factor * drawn, drawn)


def block_scale(stream_key, dims, cuts, smallest, high):
    gain = 1.0
    for dim, shards_of in cuts:
        heights = jax.random.uniform(jax.random.fold_in(jax.random.fold_in(stream_key, 6), dim), (shards_of,), jnp.float32, smallest / len(cuts), high / len(cuts))
        gain = gain * jnp.repeat(jnp.exp(heights), dims[dim] // shards_of).reshape((-1,) + (1,) * (len(dims) - 1 - dim))
    return gain


def deal_out(key, own, number, rows, amount, top, most, lean):
    sequence = jax.random.permutation(key, amount)
    heavy_load, usual = shares(amount, rows * top, most, lean, True), shares(amount, rows * top, most, lean, False)
    places = jnp.arange(amount)

    def named(lengths, turn):
        used = int((lengths > 0).sum())
        fixed = max(1, used // 4)
        shifted = fixed + (places - fixed + turn * (used - fixed)) % max(1, amount - fixed)
        return jnp.zeros((amount,), jnp.int32).at[sequence[jnp.where(places < fixed, places, shifted)]].set(jnp.asarray(lengths, jnp.int32))

    lengths = jnp.where(number % 4 == 0, named(heavy_load, number // 4), named(usual, number - number // 4 - 1))
    mixed = jax.random.permutation(jax.random.fold_in(own, 3), amount)
    source_of, receiver = mixed[0:amount // 2 * 2:2], mixed[1:amount // 2 * 2:2]
    margin = jnp.minimum(lengths[source_of] - 1, most - lengths[receiver]) // 2
    margin = jnp.where((source_of == sequence[0]) | (receiver == sequence[0]) | (lengths[receiver] == 0), 0, jnp.maximum(margin, 0))
    shifted = jax.random.randint(jax.random.fold_in(own, 4), (amount // 2,), 0, 1 << 20) % (margin + 1)
    lengths = lengths.at[source_of].add(-shifted).at[receiver].add(shifted)
    items = jnp.searchsorted(jnp.cumsum(lengths), jnp.arange(rows * top), side="right").astype(jnp.int32)
    listing = items.reshape(top, rows).T
    listing = listing[jax.random.permutation(jax.random.fold_in(own, 1), rows)]
    turn = jax.random.randint(jax.random.fold_in(own, 2), (rows, 1), 0, top)
    return jnp.take_along_axis(listing, (jnp.arange(top)[None, :] + turn) % top, axis=1)


def shares(amount, total, limit, slope, full):
    weights = [(1 << 20) // math.isqrt(grade ** slope) + 1 for grade in range(1, amount + 1)]
    largest = limit if full else min(limit, max(-(-total // amount), total * weights[0] // sum(weights)))
    least = 1 if total - largest >= amount - 1 else 0
    holding, spare = [largest] + [least] * (amount - 1), total - largest - least * (amount - 1)
    while spare > 0:
        candidates = [i for i in range(1, amount) if holding[i] < largest] or [i for i in range(1, amount) if holding[i] < limit]
        pool, left = sum([weights[i] for i in candidates]), spare
        for i in candidates:
            addition = min(limit - holding[i], max(1, left * weights[i] // pool), spare)
            holding[i] = holding[i] + addition
            spare = spare - addition
    return np.array(holding)


def noise(key, dims, spread, limit, shards=(), kind=jnp.bfloat16):
    values = spread * jax.random.normal(key, dims, jnp.float32)
    if shards:
        values = values * block_scale(key, dims, shards, -0.22, 0.18)
    return jnp.clip(values, -limit, limit).astype(kind)


def noise_with(own_key, shape, scale, limit, split, heavy, kind=jnp.bfloat16):
    values = scale * jax.random.normal(own_key, shape, jnp.float32)
    if split:
        values = values * block_scale(own_key, shape, split, -0.22, 0.18)
    return jnp.clip(strengthened(values, jax.random.fold_in(own_key, 3), *heavy), -limit, limit).astype(kind)


def setup_inputs(seed: int = 0) -> dict:
    key_list = jax.random.split(jax.random.key(seed), 8)
    tokens = noise(key_list[0], (TOKENS, D), 1.0, 6.0, ((0, 256),))
    routes_keys = jax.random.split(jax.random.fold_in(key_list[1], 1), TOKENS // TOK_DEV)
    routes_turns = jax.random.permutation(jax.random.fold_in(key_list[1], 3), TOKENS // TOK_DEV)
    routes = jax.vmap(lambda own, number: deal_out(jax.random.fold_in(key_list[1], 2), own, number, TOK_DEV, EXPERTS, TOP, CAP, 2))(routes_keys, routes_turns).reshape((TOKENS, TOP))
    route_gains = jnp.clip(jnp.exp(math.log(1.0) - 2.3025851 * jax.random.uniform(key_list[2], (TOKENS, TOP), jnp.float32) ** block_scale(key_list[2], (TOKENS, TOP), ((0, 256),), -0.2, 0.2)), 0.1, 1.0)
    cotangent = noise_with(key_list[3], (TOKENS, D), 1.0, 24.0, ((0, 256),), (0, 1, 256, 6.0))
    w_gate = noise(key_list[4], (EXPERTS, D, FF), D ** -0.5, 0.125, ((0, 16),))
    w_up = noise(key_list[5], (EXPERTS, D, FF), D ** -0.5, 0.125, ((0, 16),))
    w_down = noise(key_list[6], (EXPERTS, D, FF), FF ** -0.5, 0.21875, ((0, 16),))
    return dict(tokens=tokens, routes=routes, route_gains=route_gains, cotangent=cotangent, w_gate=w_gate, w_up=w_up, w_down=w_down)


def slot_targets(route_rows):
    chosen = route_rows.reshape(-1).astype(jnp.int32)
    labels = jnp.arange(EXPERTS, dtype=jnp.int32)
    matches = (chosen[:, None] == labels[None, :]).astype(jnp.int32)
    before = jnp.cumsum(matches, axis=0).astype(jnp.int32) - matches
    position = jnp.sum(before * matches, axis=1).astype(jnp.int32)
    return (chosen * CAP + position).astype(jnp.int32)


def build_buffer(picked, target):
    return jnp.zeros((EXPERTS * CAP, D), jnp.bfloat16).at[target].set(picked)


def round_partial(value):
    return lax.optimization_barrier(value.astype(jnp.bfloat16)).astype(jnp.float32)


def reference(tokens, routes, route_gains, cotangent, w_gate, w_up, w_down):
    gate_full = w_gate.astype(jnp.float32)
    up_full = w_up.astype(jnp.float32)
    down_full = w_down.astype(jnp.float32)
    tok_groups = tokens.reshape(N_DP, N_EXPERT, TOK_DEV, D)
    route_groups = routes.reshape(N_DP, N_EXPERT, TOK_DEV, TOP)
    gain_groups = route_gains.reshape(N_DP, N_EXPERT, TOK_DEV, TOP)
    cot_groups = cotangent.reshape(N_DP, N_EXPERT, TOK_DEV, D)

    def group_pass(carry, group):
        tok_grp, route_grp, gain_grp, cot_grp = group
        targets = jax.vmap(slot_targets)(route_grp)
        picked = jnp.repeat(tok_grp, TOP, axis=1)
        d_out = (gain_grp.reshape(N_EXPERT, TOK_DEV * TOP, 1) * jnp.repeat(cot_grp, TOP, axis=1).astype(jnp.float32)).astype(jnp.bfloat16)
        sent_rows = jax.vmap(build_buffer)(picked, targets)
        sent_cots = jax.vmap(build_buffer)(d_out, targets)

        def arrange(buffer):
            return buffer.reshape(N_EXPERT, EXPERTS, CAP, D).transpose(1, 0, 2, 3).reshape(EXPERTS, N_EXPERT * CAP, D)

        arrived = arrange(sent_rows).astype(jnp.float32)
        arrived_cot = arrange(sent_cots).astype(jnp.float32)
        pre_gate = jnp.einsum("erd,edf->erf", arrived, gate_full)
        pre_up = jnp.einsum("erd,edf->erf", arrived, up_full)
        sigma_gate = jax.nn.sigmoid(pre_gate)
        activated = pre_gate * sigma_gate
        hidden = (activated * pre_up).astype(jnp.bfloat16)
        produced = jnp.einsum("erf,edf->erd", hidden.astype(jnp.float32), down_full).astype(jnp.bfloat16)
        d_hidden = jnp.einsum("erd,edf->erf", arrived_cot, down_full)
        d_gate = (d_hidden * pre_up * (sigma_gate * (1.0 + pre_gate * (1.0 - sigma_gate)))).astype(jnp.bfloat16)
        d_up = (d_hidden * activated).astype(jnp.bfloat16)
        d_pick = (jnp.einsum("erf,edf->erd", d_gate.astype(jnp.float32), gate_full)
                  + jnp.einsum("erf,edf->erd", d_up.astype(jnp.float32), up_full)).astype(jnp.bfloat16)
        part_gate = jnp.einsum("erd,erf->edf", arrived, d_gate.astype(jnp.float32))
        part_up = jnp.einsum("erd,erf->edf", arrived, d_up.astype(jnp.float32))
        part_down = jnp.einsum("erd,erf->edf", arrived_cot, hidden.astype(jnp.float32))
        carry = (carry[0] + round_partial(part_gate), carry[1] + round_partial(part_up), carry[2] + round_partial(part_down))

        def restore(buffer):
            return buffer.reshape(EXPERTS, N_EXPERT, CAP, D).transpose(1, 0, 2, 3).reshape(N_EXPERT, EXPERTS * CAP, D)

        def take_rows(buffer, target):
            return buffer[target]

        back_out = jax.vmap(take_rows)(restore(produced), targets).astype(jnp.float32)
        back_grad = jax.vmap(take_rows)(restore(d_pick), targets).astype(jnp.float32)
        mixed = jnp.sum(gain_grp[..., None] * back_out.reshape(N_EXPERT, TOK_DEV, TOP, D), axis=2).astype(jnp.bfloat16)
        grad_rows = jnp.sum(back_grad.reshape(N_EXPERT, TOK_DEV, TOP, D), axis=2).astype(jnp.bfloat16)
        return carry, (mixed, grad_rows)

    zeros_grad = jnp.zeros((EXPERTS, D, FF), jnp.float32)
    totals, outputs = lax.scan(group_pass, (zeros_grad, zeros_grad, zeros_grad),
                               (tok_groups, route_groups, gain_groups, cot_groups))
    layer_output = outputs[0].reshape(TOKENS, D)
    input_grad = outputs[1].reshape(TOKENS, D)
    return (layer_output, input_grad, totals[0].astype(jnp.bfloat16),
            totals[1].astype(jnp.bfloat16), totals[2].astype(jnp.bfloat16))
```

```python
import jax
import jax.numpy as jnp
from jax import lax
from jax.sharding import PartitionSpec as P

SLOTS = 32


def slot_masks(routes, experts):
    rows, picks = routes.shape
    chosen = routes.T.reshape(1, -1)
    labels = lax.broadcasted_iota(jnp.int32, (experts, rows * picks), 0)
    matches = chosen == labels
    total = rows * picks
    earlier = lax.broadcasted_iota(jnp.int32, (total, total), 0) < lax.broadcasted_iota(
        jnp.int32, (total, total), 1
    )
    before = jnp.dot(
        matches.astype(jnp.bfloat16),
        earlier.astype(jnp.bfloat16),
        preferred_element_type=jnp.float32,
    )
    position = jnp.sum(jnp.where(matches, before, 0.0), axis=0).astype(jnp.int32)
    target = chosen[0] * SLOTS + position
    slots = lax.broadcasted_iota(jnp.int32, (experts * SLOTS, total), 0)
    return (slots == target[None, :]).reshape(experts * SLOTS, picks, rows)


def rows_t(left, right):
    return lax.dot_general(
        left, right, (((1,), (1,)), ((), ())), preferred_element_type=jnp.float32
    )


def outer_rows(left, right):
    return lax.dot_general(
        left, right, (((0,), (0,)), ((), ())), preferred_element_type=jnp.float32
    )


def shards(tokens, routes, route_gains, cotangent, w_gate, w_up, w_down):
    experts = lax.axis_size("expert")
    groups = lax.axis_size("dp")
    width = tokens.shape[1]
    depth = width // groups
    flip = [(a * experts + b, b * experts + a) for a in range(groups) for b in range(experts)]
    mine = lax.axis_index("dp") * depth
    hidden_units = w_gate.shape[2]

    def fetch(w):
        part = lax.dynamic_slice_in_dim(w[0], mine, depth, axis=0)
        return part

    part = jnp.concatenate([fetch(w_gate), fetch(w_up), fetch(w_down)], axis=1)
    part = lax.ppermute(part, ("dp", "expert"), flip)
    full = lax.all_gather(part, "expert", axis=0, tiled=True)
    gate_mat = full[:, :hidden_units]
    up_mat = full[:, hidden_units : 2 * hidden_units]
    down_mat = full[:, 2 * hidden_units :]

    masks = slot_masks(routes, groups)
    first = masks[:, 0, :].astype(jnp.bfloat16)
    second = masks[:, 1, :].astype(jnp.bfloat16)
    both = first + second
    gains = route_gains.T
    slot_gain = jnp.sum(jnp.where(masks, gains[None], 0.0), axis=(1, 2))
    send_tok = jnp.dot(both, tokens, preferred_element_type=jnp.float32).astype(jnp.bfloat16)
    send_cot = (
        slot_gain[:, None] * jnp.dot(both, cotangent, preferred_element_type=jnp.float32)
    ).astype(jnp.bfloat16)

    def exchange(block):
        block = block.reshape(groups, SLOTS, width)
        block = lax.all_to_all(block, "dp", split_axis=0, concat_axis=0, tiled=True)
        return block.reshape(groups * SLOTS, width)

    arrived = exchange(send_tok)
    arrived_cot = exchange(send_cot)

    pre_gate = jnp.dot(arrived, gate_mat, preferred_element_type=jnp.float32)
    pre_up = jnp.dot(arrived, up_mat, preferred_element_type=jnp.float32)
    sigma = jax.nn.sigmoid(pre_gate)
    activated = pre_gate * sigma
    hidden = (activated * pre_up).astype(jnp.bfloat16)
    d_hidden = jnp.dot(arrived_cot, down_mat, preferred_element_type=jnp.float32)
    d_gate = (d_hidden * pre_up * (sigma * (1.0 + pre_gate * (1.0 - sigma)))).astype(jnp.bfloat16)
    d_up = (d_hidden * activated).astype(jnp.bfloat16)
    partial = jnp.concatenate(
        [outer_rows(arrived, d_gate), outer_rows(arrived, d_up), outer_rows(arrived_cot, hidden)],
        axis=1,
    ).astype(jnp.bfloat16)
    summed = lax.psum_scatter(partial, "expert", scatter_dimension=0, tiled=True)
    produced = rows_t(hidden, down_mat).astype(jnp.bfloat16)
    d_pick = (rows_t(d_gate, gate_mat) + rows_t(d_up, up_mat)).astype(jnp.bfloat16)
    back_out = exchange(produced)
    back_grad = exchange(d_pick)
    layer_output = (
        gains[0][:, None] * outer_rows(first, back_out)
        + gains[1][:, None] * outer_rows(second, back_out)
    ).astype(jnp.bfloat16)
    input_grad = (outer_rows(first, back_grad) + outer_rows(second, back_grad)).astype(
        jnp.bfloat16
    )
    summed = lax.ppermute(summed, ("dp", "expert"), flip)
    grad_gate = summed[None, :, :hidden_units]
    grad_up = summed[None, :, hidden_units : 2 * hidden_units]
    grad_down = summed[None, :, 2 * hidden_units :]
    return (layer_output, input_grad, grad_gate, grad_up, grad_down)


def solution(mesh):
    rows = P(("dp", "expert"), None)
    weights = P("expert", None, None)
    shares = P("expert", "dp", None)
    return jax.shard_map(
        shards,
        mesh=mesh,
        in_specs=(rows, rows, rows, rows, weights, weights, weights),
        out_specs=(rows, rows, shares, shares, shares),
        check_vma=False,
    )
```

```python
import functools

import jax
import jax.numpy as jnp
from jax import lax
from jax.experimental import pallas as pl
from jax.experimental.pallas import tpu as pltpu
from jax.sharding import PartitionSpec as P

SLOTS = 32
LANES = 128
CHUNK = 256
QUARTERS = 4
MESH = pl.DeviceIdType.MESH
F32 = jnp.float32
BF16 = jnp.bfloat16


def slot_masks(routes, experts):
    rows, picks = routes.shape
    total = rows * picks
    chosen = routes.T.reshape(1, -1)
    labels = lax.broadcasted_iota(jnp.int32, (experts, total), 0)
    matches = chosen == labels
    earlier = lax.broadcasted_iota(jnp.int32, (total, total), 0) < lax.broadcasted_iota(
        jnp.int32, (total, total), 1
    )
    before = jnp.dot(matches.astype(BF16), earlier.astype(BF16), preferred_element_type=F32)
    position = jnp.sum(jnp.where(matches, before, 0.0), axis=0).astype(jnp.int32)
    target = (chosen[0] * SLOTS + position).reshape(picks, rows)
    slots = lax.broadcasted_iota(jnp.int32, (picks, experts * SLOTS, rows), 1)
    return slots == target[:, None, :], target


def dot(a, b):
    return jnp.dot(a, b, preferred_element_type=F32)


def dot_rows(a, b):
    return lax.dot_general(a, b, (((1,), (1,)), ((), ())), preferred_element_type=F32)


def dot_outer(a, b):
    return lax.dot_general(a, b, (((0,), (0,)), ((), ())), preferred_element_type=F32)


def moe_kernel(
    n,
    nz,
    both_ref,
    first_ref,
    second_ref,
    slot_gain_ref,
    gains_ref,
    tok_ref,
    cot_ref,
    wg_ref,
    wu_ref,
    wd_ref,
    out_ref,
    ingrad_ref,
    gg_ref,
    gu_ref,
    gd_ref,
    w_buf,
    st,
    sc,
    x_buf,
    c_buf,
    hid,
    dgate,
    dup,
    dpart,
    dx_buf,
    ch_buf,
    po,
    pg,
    bo,
    bg,
    fg,
    loc_sem,
    w_recv,
    x_recv,
    ch_recv,
    dx_recv,
    one_sem,
):
    (TS, TR, TL, CS, CR, CL, OS, OR, OL, GS, GR, GL, WS, PS, XS, HS, DS, FS, FR, FL) = range(20)
    width = tok_ref.shape[1]
    chunks = w_buf.shape[1]
    rows = n * SLOTS
    quarter = width // QUARTERS
    depth = width // n
    block = 256
    row_block = min(block, rows)

    d = lax.axis_index("dp")
    ex = lax.axis_index("expert")
    z = lax.div(ex, 2)
    c = lax.rem(ex, 2)
    sgn = 1 - 2 * c
    r = lax.rem(sgn * (z - lax.div(d, 2)) + nz, nz)
    nxt = 2 * lax.rem(z + sgn + nz, nz) + c
    prv = 2 * lax.rem(z - sgn + nz, nz) + c
    mate = ex + sgn
    native = ex == d
    rootmate = mate == d

    def remote(src, dst, send, recv, dev):
        return pltpu.make_async_remote_copy(
            src_ref=src, dst_ref=dst, send_sem=send, recv_sem=recv, device_id=dev, device_id_type=MESH
        )

    def wait_bytes(ref, sem):
        pltpu.make_async_copy(ref, ref, sem).wait()

    barrier = pltpu.get_barrier_semaphore()

    def greet(dev):
        pl.semaphore_signal(barrier, inc=1, device_id=dev, device_id_type=MESH)

    @pl.loop(1, n)
    def _(j):
        greet((lax.rem(d + j, n), ex))

    greet((d, mate))
    greet((d, nxt))
    greet((d, prv))

    @pl.when(d != ex)
    def _():
        greet((ex, mate))

    @pl.when(rootmate)
    def _():
        @pl.loop(1, n)
        def _(j):
            greet((lax.rem(d + j, n), d))

    @pl.when(native)
    def _():
        for k in range(chunks):
            for m, ref in enumerate((wg_ref, wu_ref, wd_ref)):
                for h in range(2):
                    pltpu.make_async_copy(
                        ref.at[0, :, pl.ds(CHUNK * k + LANES * h, LANES)],
                        w_buf.at[h, k, m],
                        loc_sem.at[3 * k + m],
                    ).start()

    pl.semaphore_wait(
        barrier, n + 2 + jnp.where(d != ex, 1, 0) + jnp.where(rootmate, n - 1, 0)
    )

    def slot_rows(i):
        return pl.ds(pl.multiple_of(i * SLOTS, SLOTS), SLOTS)

    def exchange(src, dst, send, recv, own):
        pltpu.make_async_copy(src.at[slot_rows(d)], dst.at[slot_rows(d)], one_sem.at[own]).start()

        @pl.loop(1, n)
        def _(j):
            t = lax.rem(d + j, n)
            remote(
                src.at[slot_rows(t)], dst.at[slot_rows(d)], one_sem.at[send], one_sem.at[recv], (t, ex)
            ).start()

    def exchanged(dst, recv, own):
        wait_bytes(dst.at[pl.ds(0, SLOTS)], one_sem.at[own])
        wait_bytes(dst.at[pl.ds(0, rows - SLOTS)], one_sem.at[recv])

    def cols(i, size=block):
        return pl.ds(pl.multiple_of(i * size, size), size)

    def piece(buf, k, m, q):
        return buf.at[k, m, pl.ds(pl.multiple_of(q * quarter, quarter), quarter)]

    def weights(k):
        @pl.loop(0, 3)
        def _(m):
            km = 3 * k + m

            @pl.when(native)
            def _():
                wait_bytes(w_buf.at[:, k, m], loc_sem.at[km])

            @pl.loop(0, QUARTERS)
            def _(q):
                i = QUARTERS * km + q
                mine = piece(w_buf.at[c], k, m, q)

                @pl.when(jnp.logical_not(native))
                def _():
                    wait_bytes(mine, w_recv.at[i])

                @pl.when(r <= nz - 2)
                def _():
                    remote(mine, mine, one_sem.at[WS], w_recv.at[i], (d, nxt)).start()

                @pl.when(native)
                def _():
                    other = piece(w_buf.at[1 - c], k, m, q)
                    remote(other, other, one_sem.at[PS], w_recv.at[i], (d, mate)).start()

            @pl.when(jnp.logical_not(rootmate))
            def _():
                half = w_buf.at[c, k, m]
                remote(half, half, one_sem.at[XS], x_recv.at[km], (d, mate)).start()

    def swapped(k):
        @pl.when(jnp.logical_not(native))
        def _():
            @pl.loop(0, 3)
            def _(m):
                wait_bytes(w_buf.at[1 - c, k, m], x_recv.at[3 * k + m])

    def mat(k, m):
        return jnp.concatenate([w_buf[0, k, m], w_buf[1, k, m]], axis=1)

    def hidden_units(k):
        @pl.loop(0, rows // row_block)
        def _(i):
            sl = cols(i, row_block)
            x = x_buf[sl, :]
            gate = dot(x, mat(k, 0))
            up = dot(x, mat(k, 1))
            sigma = jax.nn.sigmoid(gate)
            act = gate * sigma
            hid[k, sl, :] = (act * up).astype(BF16)
            dh = dot(c_buf[sl, :], mat(k, 2))
            dgate[k, sl, :] = (dh * up * (sigma * (1.0 + gate * (1.0 - sigma)))).astype(BF16)
            dup[k, sl, :] = (dh * act).astype(BF16)

    def outer(k):
        @pl.loop(0, width // block)
        def _(i):
            sl = cols(i)
            pair = jnp.concatenate([dgate[k], dup[k]], axis=1)
            both = dot_outer(x_buf[:, sl], pair).astype(BF16)
            down = dot_outer(c_buf[:, sl], hid[k]).astype(BF16)
            dpart[0, k, 0, sl, :] = both[:, :LANES]
            dpart[1, k, 0, sl, :] = both[:, LANES:CHUNK]
            dpart[0, k, 1, sl, :] = both[:, CHUNK : CHUNK + LANES]
            dpart[1, k, 1, sl, :] = both[:, CHUNK + LANES :]
            dpart[0, k, 2, sl, :] = down[:, :LANES]
            dpart[1, k, 2, sl, :] = down[:, LANES:]

        remote(dpart.at[1 - c, k], dx_buf.at[k], one_sem.at[DS], dx_recv.at[k], (d, mate)).start()

    def rows_of(k, m, sl):
        return jnp.concatenate([w_buf[0, k, m, sl, :], w_buf[1, k, m, sl, :]], axis=1)

    def produce():
        @pl.loop(0, width // block)
        def _(i):
            sl = cols(i)
            acc = dot_rows(hid[0], rows_of(0, 2, sl))
            for k in range(1, chunks):
                acc += dot_rows(hid[k], rows_of(k, 2, sl))
            po[:, sl] = acc.astype(BF16)

    def pick_grads():
        @pl.loop(0, width // block)
        def _(i):
            sl = cols(i)
            acc = dot_rows(dgate[0], rows_of(0, 0, sl))
            acc += dot_rows(dup[0], rows_of(0, 1, sl))
            for k in range(1, chunks):
                acc += dot_rows(dgate[k], rows_of(k, 0, sl))
                acc += dot_rows(dup[k], rows_of(k, 1, sl))
            pg[:, sl] = acc.astype(BF16)

    def chain(k):
        wait_bytes(dx_buf.at[k], dx_recv.at[k])

        @pl.loop(0, 3)
        def _(m):
            km = 3 * k + m

            @pl.loop(0, QUARTERS)
            def _(q):
                i = QUARTERS * km + q
                sl = pl.ds(pl.multiple_of(q * quarter, quarter), quarter)
                mine = piece(dpart.at[c], k, m, q)
                there = piece(ch_buf, k, m, q)
                own = dpart[c, k, m, sl, :].astype(F32) + dx_buf[k, m, sl, :].astype(F32)

                @pl.when(r == 1)
                def _():
                    dpart[c, k, m, sl, :] = own.astype(BF16)

                @pl.when(r != 1)
                def _():
                    wait_bytes(there, ch_recv.at[i])
                    dpart[c, k, m, sl, :] = (own + ch_buf[k, m, sl, :].astype(F32)).astype(BF16)

                @pl.when(r != 0)
                def _():
                    remote(mine, there, one_sem.at[HS], ch_recv.at[i], (d, nxt)).start()

            @pl.when(r == 0)
            def _():
                def share(t):
                    return dpart.at[c, k, m, pl.ds(pl.multiple_of(t * depth, depth), depth)]

                @pl.when(native)
                def _():
                    pltpu.make_async_copy(share(d), fg.at[c, k, m], one_sem.at[FL]).start()

                @pl.when(rootmate)
                def _():
                    remote(
                        share(d), fg.at[c, k, m], one_sem.at[FS], one_sem.at[FR], (d, d)
                    ).start()

                @pl.loop(1, n)
                def _(j):
                    t = lax.rem(d + j, n)
                    remote(
                        share(t), fg.at[c, k, m], one_sem.at[FS], one_sem.at[FR], (t, d)
                    ).start()

    @pl.loop(0, width // 512)
    def _(i):
        sl = cols(i, 512)
        st[:, sl] = dot(both_ref[...], tok_ref[:, sl]).astype(BF16)

    exchange(st, x_buf, TS, TR, TL)

    @pl.loop(0, width // 512)
    def _(i):
        sl = cols(i, 512)
        sc[:, sl] = (slot_gain_ref[...] * dot(both_ref[...], cot_ref[:, sl])).astype(BF16)

    exchange(sc, c_buf, CS, CR, CL)

    @pl.loop(0, chunks)
    def _(k):
        weights(k)

    exchanged(x_buf, TR, TL)
    exchanged(c_buf, CR, CL)

    @pl.loop(0, chunks)
    def _(k):
        swapped(k)
        hidden_units(k)
        outer(k)

    produce()
    exchange(po, bo, OS, OR, OL)
    pick_grads()
    exchange(pg, bg, GS, GR, GL)

    @pl.loop(0, chunks)
    def _(k):
        chain(k)

    exchanged(bo, OR, OL)
    gain = gains_ref[...]

    @pl.loop(0, width // 512)
    def _(i):
        sl = cols(i, 512)
        got = bo[:, sl]
        out_ref[:, sl] = (
            gain[:, 0:1] * dot(first_ref[...], got) + gain[:, 1:2] * dot(second_ref[...], got)
        ).astype(BF16)

    exchanged(bg, GR, GL)

    @pl.loop(0, width // 512)
    def _(i):
        sl = cols(i, 512)
        got = bg[:, sl]
        ingrad_ref[:, sl] = (dot(first_ref[...], got) + dot(second_ref[...], got)).astype(BF16)

    @pl.when(native)
    def _():
        wait_bytes(fg.at[0], one_sem.at[FL])
        wait_bytes(fg.at[0], one_sem.at[FR])
        wait_bytes(dpart.at[0, :, :, pl.ds(0, width - depth)], one_sem.at[FS])

    @pl.when(jnp.logical_not(native))
    def _():
        wait_bytes(fg, one_sem.at[FR])

    @pl.when(rootmate)
    def _():
        wait_bytes(dpart.at[0], one_sem.at[FS])

    for k in range(chunks):
        for h in range(2):
            sl = slice(CHUNK * k + LANES * h, CHUNK * k + LANES * (h + 1))
            gg_ref[0, :, sl] = fg[h, k, 0]
            gu_ref[0, :, sl] = fg[h, k, 1]
            gd_ref[0, :, sl] = fg[h, k, 2]

    for send, buf in ((TS, st), (CS, sc), (OS, po), (GS, pg)):
        wait_bytes(buf.at[pl.ds(0, rows - SLOTS)], one_sem.at[send])

    @pl.when(r <= nz - 2)
    def _():
        wait_bytes(w_buf.at[0], one_sem.at[WS])

    @pl.when(native)
    def _():
        wait_bytes(w_buf.at[0], one_sem.at[PS])

    @pl.when(jnp.logical_not(rootmate))
    def _():
        wait_bytes(w_buf.at[0], one_sem.at[XS])

    @pl.when(r != 0)
    def _():
        wait_bytes(ch_buf, one_sem.at[HS])

    wait_bytes(dx_buf, one_sem.at[DS])


def shards(n, tokens, routes, route_gains, cotangent, w_gate, w_up, w_down):
    width = tokens.shape[1]
    units = w_gate.shape[2]
    chunks = units // CHUNK
    count = tokens.shape[0]
    depth = width // n
    rows = n * SLOTS

    masks, target = slot_masks(routes, n)
    both = (masks[0] | masks[1]).astype(BF16)
    gains = route_gains.T
    slot_gain = jnp.sum(jnp.where(masks, gains[:, None, :], 0.0), axis=(0, 2))[:, None]
    slots = lax.broadcasted_iota(jnp.int32, (count, rows), 1)
    first = (slots == target[0][:, None]).astype(BF16)
    second = (slots == target[1][:, None]).astype(BF16)

    vmem = pl.BlockSpec(memory_space=pltpu.VMEM)
    anywhere = pl.BlockSpec(memory_space=pl.ANY)
    sem = pltpu.SemaphoreType.DMA
    share = jax.ShapeDtypeStruct((1, depth, units), BF16)
    row_out = jax.ShapeDtypeStruct((count, width), BF16)
    landed = pltpu.VMEM((rows, width), BF16)
    acts = pltpu.VMEM((chunks, rows, CHUNK), BF16)
    half = pltpu.VMEM((chunks, 3, width, LANES), BF16)
    halves = pltpu.VMEM((2, chunks, 3, width, LANES), BF16)
    return pl.pallas_call(
        functools.partial(moe_kernel, n, n // 2),
        out_shape=(row_out, row_out, share, share, share),
        in_specs=[vmem] * 7 + [anywhere] * 3,
        out_specs=(vmem,) * 5,
        scratch_shapes=[
            halves,
            landed,
            landed,
            landed,
            landed,
            acts,
            acts,
            acts,
            halves,
            half,
            half,
            landed,
            landed,
            landed,
            landed,
            pltpu.VMEM((2, chunks, 3, depth, LANES), BF16),
            sem((3 * chunks,)),
            sem((3 * chunks * QUARTERS,)),
            sem((3 * chunks,)),
            sem((3 * chunks * QUARTERS,)),
            sem((chunks,)),
            sem((20,)),
        ],
        compiler_params=pltpu.CompilerParams(
            collective_id=0, has_side_effects=True, vmem_limit_bytes=60 * 2**20
        ),
    )(both, first, second, slot_gain, route_gains, tokens, cotangent, w_gate, w_up, w_down)


def solution(mesh):
    rows = P(("dp", "expert"), None)
    weights = P("expert", None, None)
    shares = P("expert", "dp", None)
    return jax.shard_map(
        functools.partial(shards, mesh.shape["dp"]),
        mesh=mesh,
        in_specs=(rows, rows, rows, rows, weights, weights, weights),
        out_specs=(rows, rows, shares, shares, shares),
        check_vma=False,
    )
```

```python
import functools
import math

import jax
import jax.numpy as jnp
from jax import lax
from jax.experimental import pallas as pl
from jax.experimental.pallas import tpu as pltpu
from jax.sharding import PartitionSpec as P

SLOTS = 32
LANES = 128
CHUNK = 256
QUARTERS = 8
MESH = pl.DeviceIdType.MESH
OFFSETS = (
    (1, 0), (3, 0), (0, 1), (0, 3), (1, 1), (3, 3), (1, 3), (3, 1),
    (2, 0), (0, 2), (2, 2), (2, 1), (1, 2), (2, 3), (3, 2),
)
F32 = jnp.float32
BF16 = jnp.bfloat16


def dot(a, b):
    return jnp.dot(a, b, preferred_element_type=F32)


def dot_rows(a, b):
    return lax.dot_general(a, b, (((1,), (1,)), ((), ())), preferred_element_type=F32)


def dot_outer(a, b):
    return lax.dot_general(a, b, (((0,), (0,)), ((), ())), preferred_element_type=F32)


def moe_kernel(
    n,
    nz,
    routes_ref,
    gains_ref,
    tok_ref,
    cot_ref,
    wg_ref,
    wu_ref,
    wd_ref,
    out_ref,
    ingrad_ref,
    gg_ref,
    gu_ref,
    gd_ref,
    pick_a,
    pick_b,
    w_buf,
    st,
    sc,
    x_buf,
    c_buf,
    hid,
    dgate,
    dup,
    dpart,
    dx_buf,
    ch_buf,
    po,
    pg,
    bo,
    bg,
    fg,
    loc_sem,
    w_recv,
    x_recv,
    ch_recv,
    dx_recv,
    one_sem,
):
    (TS, TR, TL, CS, CR, CL, OS, OR, OL, GS, GR, GL, WS, PS, XS, HS, DS, FS, FR, FL) = range(20)
    width = tok_ref.shape[1]
    chunks = w_buf.shape[1]
    rows = n * SLOTS
    quarter = width // QUARTERS
    depth = width // n
    block = 256
    row_block = min(block, rows)

    d = lax.axis_index("dp")
    ex = lax.axis_index("expert")
    z = lax.div(ex, 2)
    c = lax.rem(ex, 2)
    sgn = 1 - 2 * c
    r = lax.rem(sgn * (z - lax.div(d, 2)) + nz, nz)
    nxt = 2 * lax.rem(z + sgn + nz, nz) + c
    prv = 2 * lax.rem(z - sgn + nz, nz) + c
    mate = ex + sgn
    native = ex == d
    rootmate = mate == d
    side = math.isqrt(n)
    others = [
        lax.rem(lax.div(d, side) + a, side) * side + lax.rem(lax.rem(d, side) + b, side)
        for a, b in OFFSETS
        if a < side and b < side
    ]

    def remote(src, dst, send, recv, dev):
        return pltpu.make_async_remote_copy(
            src_ref=src, dst_ref=dst, send_sem=send, recv_sem=recv, device_id=dev, device_id_type=MESH
        )

    def wait_bytes(ref, sem):
        pltpu.make_async_copy(ref, ref, sem).wait()

    barrier = pltpu.get_barrier_semaphore()

    def greet(dev):
        pl.semaphore_signal(barrier, inc=1, device_id=dev, device_id_type=MESH)

    @pl.loop(1, n)
    def _(j):
        greet((lax.rem(d + j, n), ex))

    greet((d, mate))
    greet((d, nxt))
    greet((d, prv))

    @pl.when(d != ex)
    def _():
        greet((ex, mate))

    @pl.when(rootmate)
    def _():
        @pl.loop(1, n)
        def _(j):
            greet((lax.rem(d + j, n), d))

    @pl.when(native)
    def _():
        for k in range(chunks):
            for m, ref in enumerate((wg_ref, wu_ref, wd_ref)):
                for h in range(2):
                    pltpu.make_async_copy(
                        ref.at[0, :, pl.ds(CHUNK * k + LANES * h, LANES)],
                        w_buf.at[h, k, m],
                        loc_sem.at[3 * k + m],
                    ).start()

    count = tok_ref.shape[0]

    def iota(shape, dim):
        return lax.broadcasted_iota(jnp.int32, shape, dim)

    def ones(mask):
        return jnp.where(mask, 1.0, 0.0).astype(BF16)

    names = [routes_ref[k : k + 1, :] for k in range(2)]
    named = [name == iota((n, count), 0) for name in names]
    square = (count, count)
    before = dot(ones(named[0]) + ones(named[1]), ones(iota(square, 0) < iota(square, 1)))
    for buf, name, match in zip((pick_a, pick_b), names, named):
        place = jnp.sum(jnp.where(match, before, 0.0), axis=0, keepdims=True).astype(jnp.int32)
        buf[...] = ones(iota((rows, count), 0) == name * SLOTS + place)
    gain_a, gain_b = [
        jnp.sum(
            jnp.where(iota(square, 0) == iota(square, 1), gains_ref[k : k + 1, :], 0.0),
            axis=1,
            keepdims=True,
        )
        for k in range(2)
    ]

    pl.semaphore_wait(
        barrier, n + 2 + jnp.where(d != ex, 1, 0) + jnp.where(rootmate, n - 1, 0)
    )

    def slot_rows(i):
        return pl.ds(pl.multiple_of(i * SLOTS, SLOTS), SLOTS)

    def exchange(src, dst, send, recv, own):
        pltpu.make_async_copy(src.at[slot_rows(d)], dst.at[slot_rows(d)], one_sem.at[own]).start()

        for t in others:
            remote(
                src.at[slot_rows(t)], dst.at[slot_rows(d)], one_sem.at[send], one_sem.at[recv], (t, ex)
            ).start()

    def exchanged(dst, recv, own):
        wait_bytes(dst.at[pl.ds(0, SLOTS)], one_sem.at[own])
        wait_bytes(dst.at[pl.ds(0, rows - SLOTS)], one_sem.at[recv])

    def cols(i, size=block):
        return pl.ds(pl.multiple_of(i * size, size), size)

    def piece(buf, k, m, q):
        return buf.at[k, m, pl.ds(pl.multiple_of(q * quarter, quarter), quarter)]

    def weights(km):
        k = lax.div(km, 3)
        m = lax.rem(km, 3)

        @pl.when(native)
        def _():
            wait_bytes(w_buf.at[:, k, m], loc_sem.at[km])

        @pl.loop(0, QUARTERS)
        def _(q):
            i = QUARTERS * km + q
            mine = piece(w_buf.at[c], k, m, q)

            @pl.when(jnp.logical_not(native))
            def _():
                wait_bytes(mine, w_recv.at[i])

            @pl.when(r <= nz - 2)
            def _():
                remote(mine, mine, one_sem.at[WS], w_recv.at[i], (d, nxt)).start()

            @pl.when(native)
            def _():
                other = piece(w_buf.at[1 - c], k, m, q)
                remote(other, other, one_sem.at[PS], w_recv.at[i], (d, mate)).start()

        @pl.when(jnp.logical_not(rootmate))
        def _():
            half = w_buf.at[c, k, m]
            remote(half, half, one_sem.at[XS], x_recv.at[km], (d, mate)).start()

    def swapped(k):
        @pl.when(jnp.logical_not(native))
        def _():
            @pl.loop(0, 3)
            def _(m):
                wait_bytes(w_buf.at[1 - c, k, m], x_recv.at[3 * k + m])

    def mat(k, m):
        return jnp.concatenate([w_buf[0, k, m], w_buf[1, k, m]], axis=1)

    def hidden_units(k):
        @pl.loop(0, rows // row_block)
        def _(i):
            sl = cols(i, row_block)
            x = x_buf[sl, :]
            gate = dot(x, mat(k, 0))
            up = dot(x, mat(k, 1))
            sigma = jax.nn.sigmoid(gate)
            act = gate * sigma
            hid[k, sl, :] = (act * up).astype(BF16)
            dh = dot(c_buf[sl, :], mat(k, 2))
            dgate[k, sl, :] = (dh * up * (sigma * (1.0 + gate * (1.0 - sigma)))).astype(BF16)
            dup[k, sl, :] = (dh * act).astype(BF16)

    def outer(k):
        @pl.loop(0, width // block)
        def _(i):
            sl = cols(i)
            pair = jnp.concatenate([dgate[k], dup[k]], axis=1)
            both = dot_outer(x_buf[:, sl], pair).astype(BF16)
            down = dot_outer(c_buf[:, sl], hid[k]).astype(BF16)
            dpart[0, k, 0, sl, :] = both[:, :LANES]
            dpart[1, k, 0, sl, :] = both[:, LANES:CHUNK]
            dpart[0, k, 1, sl, :] = both[:, CHUNK : CHUNK + LANES]
            dpart[1, k, 1, sl, :] = both[:, CHUNK + LANES :]
            dpart[0, k, 2, sl, :] = down[:, :LANES]
            dpart[1, k, 2, sl, :] = down[:, LANES:]

        remote(dpart.at[1 - c, k], dx_buf.at[k], one_sem.at[DS], dx_recv.at[k], (d, mate)).start()

    def rows_of(k, m, sl):
        return jnp.concatenate([w_buf[0, k, m, sl, :], w_buf[1, k, m, sl, :]], axis=1)

    def produce():
        @pl.loop(0, width // block)
        def _(i):
            sl = cols(i)
            acc = dot_rows(hid[0], rows_of(0, 2, sl))
            for k in range(1, chunks):
                acc += dot_rows(hid[k], rows_of(k, 2, sl))
            po[:, sl] = acc.astype(BF16)

    def pick_grads():
        @pl.loop(0, width // block)
        def _(i):
            sl = cols(i)
            acc = dot_rows(dgate[0], rows_of(0, 0, sl))
            acc += dot_rows(dup[0], rows_of(0, 1, sl))
            for k in range(1, chunks):
                acc += dot_rows(dgate[k], rows_of(k, 0, sl))
                acc += dot_rows(dup[k], rows_of(k, 1, sl))
            pg[:, sl] = acc.astype(BF16)

    def chain(k, m):
        if m == 0:
            wait_bytes(dx_buf.at[k], dx_recv.at[k])
        km = 3 * k + m

        @pl.loop(0, QUARTERS)
        def _(q):
            i = QUARTERS * km + q
            sl = pl.ds(pl.multiple_of(q * quarter, quarter), quarter)
            mine = piece(dpart.at[c], k, m, q)
            there = piece(ch_buf, k, m, q)
            own = dpart[c, k, m, sl, :].astype(F32) + dx_buf[k, m, sl, :].astype(F32)

            @pl.when(r == 1)
            def _():
                dpart[c, k, m, sl, :] = own.astype(BF16)

            @pl.when(r != 1)
            def _():
                wait_bytes(there, ch_recv.at[i])
                dpart[c, k, m, sl, :] = (own + ch_buf[k, m, sl, :].astype(F32)).astype(BF16)

            @pl.when(r != 0)
            def _():
                remote(mine, there, one_sem.at[HS], ch_recv.at[i], (d, nxt)).start()

        @pl.when(r == 0)
        def _():
            def share(t):
                return dpart.at[c, k, m, pl.ds(pl.multiple_of(t * depth, depth), depth)]

            @pl.when(native)
            def _():
                pltpu.make_async_copy(share(d), fg.at[c, k, m], one_sem.at[FL]).start()

            @pl.when(rootmate)
            def _():
                remote(share(d), fg.at[c, k, m], one_sem.at[FS], one_sem.at[FR], (d, d)).start()

            for t in others:
                remote(share(t), fg.at[c, k, m], one_sem.at[FS], one_sem.at[FR], (t, d)).start()

    @pl.loop(0, width // 512)
    def _(i):
        sl = cols(i, 512)
        st[:, sl] = dot(pick_a[...] + pick_b[...], tok_ref[:, sl]).astype(BF16)

    exchange(st, x_buf, TS, TR, TL)

    @pl.loop(0, width // 512)
    def _(i):
        sl = cols(i, 512)
        cot = cot_ref[:, sl].astype(F32)
        sc[:, sl] = (
            dot(pick_a[...], (gain_a * cot).astype(BF16))
            + dot(pick_b[...], (gain_b * cot).astype(BF16))
        ).astype(BF16)

    exchange(sc, c_buf, CS, CR, CL)

    middle = nz // 2
    early = r < middle
    late = jnp.logical_not(early)
    near = jnp.logical_and(r >= 1, r < middle)
    mid = jnp.logical_and(r >= middle, r <= middle + 1)
    far = jnp.logical_or(r == 0, r > middle + 1)

    @pl.loop(0, 6)
    def _(km):
        weights(km)

    @pl.when(early)
    def _():
        @pl.loop(6, 9)
        def _(km):
            weights(km)

    exchanged(x_buf, TR, TL)
    exchanged(c_buf, CR, CL)
    swapped(0)
    hidden_units(0)
    pl.when(late)(lambda: weights(6))
    outer(0)
    pl.when(late)(lambda: weights(7))
    swapped(1)
    hidden_units(1)
    pl.when(late)(lambda: weights(8))
    outer(1)
    pl.when(near)(lambda: chain(0, 0))
    swapped(2)
    hidden_units(2)
    pl.when(near)(lambda: chain(0, 1))
    produce()
    exchange(po, bo, OS, OR, OL)
    pl.when(mid)(lambda: chain(0, 0))
    pick_grads()
    exchange(pg, bg, GS, GR, GL)
    pl.when(mid)(lambda: chain(0, 1))

    @pl.when(far)
    def _():
        chain(0, 0)
        chain(0, 1)

    chain(0, 2)
    outer(2)
    for k in range(1, chunks):
        for m in range(3):
            chain(k, m)

    exchanged(bo, OR, OL)

    @pl.loop(0, width // 512)
    def _(i):
        sl = cols(i, 512)
        got = bo[:, sl]
        out_ref[:, sl] = (
            gain_a * dot_outer(pick_a[...], got) + gain_b * dot_outer(pick_b[...], got)
        ).astype(BF16)

    exchanged(bg, GR, GL)

    @pl.loop(0, width // 512)
    def _(i):
        sl = cols(i, 512)
        got = bg[:, sl]
        ingrad_ref[:, sl] = (
            dot_outer(pick_a[...], got) + dot_outer(pick_b[...], got)
        ).astype(BF16)

    @pl.when(native)
    def _():
        wait_bytes(fg.at[0], one_sem.at[FL])
        wait_bytes(fg.at[0], one_sem.at[FR])
        wait_bytes(dpart.at[0, :, :, pl.ds(0, width - depth)], one_sem.at[FS])

    @pl.when(jnp.logical_not(native))
    def _():
        wait_bytes(fg, one_sem.at[FR])

    @pl.when(rootmate)
    def _():
        wait_bytes(dpart.at[0], one_sem.at[FS])

    for k in range(chunks):
        for h in range(2):
            sl = slice(CHUNK * k + LANES * h, CHUNK * k + LANES * (h + 1))
            gg_ref[0, :, sl] = fg[h, k, 0]
            gu_ref[0, :, sl] = fg[h, k, 1]
            gd_ref[0, :, sl] = fg[h, k, 2]

    for send, buf in ((TS, st), (CS, sc), (OS, po), (GS, pg)):
        wait_bytes(buf.at[pl.ds(0, rows - SLOTS)], one_sem.at[send])

    @pl.when(r <= nz - 2)
    def _():
        wait_bytes(w_buf.at[0], one_sem.at[WS])

    @pl.when(native)
    def _():
        wait_bytes(w_buf.at[0], one_sem.at[PS])

    @pl.when(jnp.logical_not(rootmate))
    def _():
        wait_bytes(w_buf.at[0], one_sem.at[XS])

    @pl.when(r != 0)
    def _():
        wait_bytes(ch_buf, one_sem.at[HS])

    wait_bytes(dx_buf, one_sem.at[DS])


def shards(n, tokens, routes, route_gains, cotangent, w_gate, w_up, w_down):
    width = tokens.shape[1]
    units = w_gate.shape[2]
    chunks = units // CHUNK
    count = tokens.shape[0]
    depth = width // n
    rows = n * SLOTS

    vmem = pl.BlockSpec(memory_space=pltpu.VMEM)
    anywhere = pl.BlockSpec(memory_space=pl.ANY)
    sem = pltpu.SemaphoreType.DMA
    share = jax.ShapeDtypeStruct((1, depth, units), BF16)
    row_out = jax.ShapeDtypeStruct((count, width), BF16)
    landed = pltpu.VMEM((rows, width), BF16)
    acts = pltpu.VMEM((chunks, rows, CHUNK), BF16)
    half = pltpu.VMEM((chunks, 3, width, LANES), BF16)
    halves = pltpu.VMEM((2, chunks, 3, width, LANES), BF16)
    return pl.pallas_call(
        functools.partial(moe_kernel, n, n // 2),
        out_shape=(row_out, row_out, share, share, share),
        in_specs=[vmem] * 4 + [anywhere] * 3,
        out_specs=(vmem,) * 5,
        scratch_shapes=[
            pltpu.VMEM((rows, count), BF16),
            pltpu.VMEM((rows, count), BF16),
            halves,
            landed,
            landed,
            landed,
            landed,
            acts,
            acts,
            acts,
            halves,
            half,
            half,
            landed,
            landed,
            landed,
            landed,
            pltpu.VMEM((2, chunks, 3, depth, LANES), BF16),
            sem((3 * chunks,)),
            sem((3 * chunks * QUARTERS,)),
            sem((3 * chunks,)),
            sem((3 * chunks * QUARTERS,)),
            sem((chunks,)),
            sem((20,)),
        ],
        compiler_params=pltpu.CompilerParams(
            collective_id=0, has_side_effects=True, vmem_limit_bytes=60 * 2**20
        ),
    )(routes.T, route_gains.T, tokens, cotangent, w_gate, w_up, w_down)


def solution(mesh):
    rows = P(("dp", "expert"), None)
    weights = P("expert", None, None)
    shares = P("expert", "dp", None)
    return jax.shard_map(
        functools.partial(shards, mesh.shape["dp"]),
        mesh=mesh,
        in_specs=(rows, rows, rows, rows, weights, weights, weights),
        out_specs=(rows, rows, shares, shares, shares),
        check_vma=False,
    )
```

```python
import functools
import math

import jax
import jax.numpy as jnp
from jax import lax
from jax.experimental import pallas as pl
from jax.experimental.pallas import tpu as pltpu
from jax.sharding import PartitionSpec as P

SLOTS = 32
LANES = 128
CHUNK = 256
QUARTERS = 8
MESH = pl.DeviceIdType.MESH
OFFSETS = (
    (1, 0), (3, 0), (0, 1), (0, 3), (1, 1), (3, 3), (1, 3), (3, 1),
    (2, 0), (0, 2), (2, 2), (2, 1), (1, 2), (2, 3), (3, 2),
)
F32 = jnp.float32
BF16 = jnp.bfloat16


def dot(a, b):
    return jnp.dot(a, b, preferred_element_type=F32)


def dot_rows(a, b):
    return lax.dot_general(a, b, (((1,), (1,)), ((), ())), preferred_element_type=F32)


def dot_outer(a, b):
    return lax.dot_general(a, b, (((0,), (0,)), ((), ())), preferred_element_type=F32)


def moe_kernel(
    n,
    nz,
    routes_ref,
    gains_ref,
    tok_ref,
    cot_ref,
    wg_ref,
    wu_ref,
    wd_ref,
    out_ref,
    ingrad_ref,
    gg_ref,
    gu_ref,
    gd_ref,
    pick_a,
    pick_b,
    w_buf,
    st,
    sc,
    x_buf,
    c_buf,
    hid,
    dgate,
    dup,
    dpart,
    dx_buf,
    ch_buf,
    po,
    pg,
    bo,
    bg,
    fg,
    loc_sem,
    w_recv,
    x_recv,
    ch_recv,
    dx_recv,
    one_sem,
):
    (TS, TR, TL, CS, CR, CL, OS, OR, OL, GS, GR, GL, WS, PS, XS, HS, DS, FS, FR, FL) = range(20)
    width = tok_ref.shape[1]
    chunks = w_buf.shape[1]
    rows = n * SLOTS
    quarter = width // QUARTERS
    depth = width // n
    block = 256
    row_block = min(block, rows)

    d = lax.axis_index("dp")
    ex = lax.axis_index("expert")
    z = lax.div(ex, 2)
    c = lax.rem(ex, 2)
    sgn = 1 - 2 * c
    r = lax.rem(sgn * (z - lax.div(d, 2)) + nz, nz)
    nxt = 2 * lax.rem(z + sgn + nz, nz) + c
    prv = 2 * lax.rem(z - sgn + nz, nz) + c
    mate = ex + sgn
    native = ex == d
    rootmate = mate == d
    side = math.isqrt(n)
    others = [
        lax.rem(lax.div(d, side) + a, side) * side + lax.rem(lax.rem(d, side) + b, side)
        for a, b in OFFSETS
        if a < side and b < side
    ]

    def remote(src, dst, send, recv, dev):
        return pltpu.make_async_remote_copy(
            src_ref=src, dst_ref=dst, send_sem=send, recv_sem=recv, device_id=dev, device_id_type=MESH
        )

    def wait_bytes(ref, sem):
        pltpu.make_async_copy(ref, ref, sem).wait()

    barrier = pltpu.get_barrier_semaphore()

    def greet(dev):
        pl.semaphore_signal(barrier, inc=1, device_id=dev, device_id_type=MESH)

    @pl.loop(1, n)
    def _(j):
        greet((lax.rem(d + j, n), ex))

    greet((d, mate))
    greet((d, nxt))
    greet((d, prv))

    @pl.when(d != ex)
    def _():
        greet((ex, mate))

    @pl.when(rootmate)
    def _():
        @pl.loop(1, n)
        def _(j):
            greet((lax.rem(d + j, n), d))

    @pl.when(native)
    def _():
        for k in range(chunks):
            for m, ref in enumerate((wg_ref, wu_ref, wd_ref)):
                for h in range(2):
                    pltpu.make_async_copy(
                        ref.at[0, :, pl.ds(CHUNK * k + LANES * h, LANES)],
                        w_buf.at[h, k, m],
                        loc_sem.at[3 * k + m],
                    ).start()

    count = tok_ref.shape[0]

    def iota(shape, dim):
        return lax.broadcasted_iota(jnp.int32, shape, dim)

    def ones(mask):
        return jnp.where(mask, 1.0, 0.0).astype(BF16)

    names = [routes_ref[k : k + 1, :] for k in range(2)]
    named = [name == iota((n, count), 0) for name in names]
    square = (count, count)
    before = dot(ones(named[0]) + ones(named[1]), ones(iota(square, 0) < iota(square, 1)))
    for buf, name, match in zip((pick_a, pick_b), names, named):
        place = jnp.sum(jnp.where(match, before, 0.0), axis=0, keepdims=True).astype(jnp.int32)
        buf[...] = ones(iota((rows, count), 0) == name * SLOTS + place)
    gain_a, gain_b = [
        jnp.sum(
            jnp.where(iota(square, 0) == iota(square, 1), gains_ref[k : k + 1, :], 0.0),
            axis=1,
            keepdims=True,
        )
        for k in range(2)
    ]

    pl.semaphore_wait(
        barrier, n + 2 + jnp.where(d != ex, 1, 0) + jnp.where(rootmate, n - 1, 0)
    )

    def slot_rows(i):
        return pl.ds(pl.multiple_of(i * SLOTS, SLOTS), SLOTS)

    def exchange(src, dst, send, recv, own):
        pltpu.make_async_copy(src.at[slot_rows(d)], dst.at[slot_rows(d)], one_sem.at[own]).start()

        for t in others:
            remote(
                src.at[slot_rows(t)], dst.at[slot_rows(d)], one_sem.at[send], one_sem.at[recv], (t, ex)
            ).start()

    def exchanged(dst, recv, own):
        wait_bytes(dst.at[pl.ds(0, SLOTS)], one_sem.at[own])
        wait_bytes(dst.at[pl.ds(0, rows - SLOTS)], one_sem.at[recv])

    def cols(i, size=block):
        return pl.ds(pl.multiple_of(i * size, size), size)

    def piece(buf, k, m, q):
        return buf.at[k, m, pl.ds(pl.multiple_of(q * quarter, quarter), quarter)]

    def weights(km):
        k = lax.div(km, 3)
        m = lax.rem(km, 3)

        @pl.when(native)
        def _():
            wait_bytes(w_buf.at[:, k, m], loc_sem.at[km])

        @pl.loop(0, QUARTERS)
        def _(q):
            i = QUARTERS * km + q
            mine = piece(w_buf.at[c], k, m, q)

            @pl.when(jnp.logical_not(native))
            def _():
                wait_bytes(mine, w_recv.at[i])

            @pl.when(r <= nz - 2)
            def _():
                remote(mine, mine, one_sem.at[WS], w_recv.at[i], (d, nxt)).start()

            @pl.when(native)
            def _():
                other = piece(w_buf.at[1 - c], k, m, q)
                remote(other, other, one_sem.at[PS], w_recv.at[i], (d, mate)).start()

        @pl.when(jnp.logical_not(rootmate))
        def _():
            half = w_buf.at[c, k, m]
            remote(half, half, one_sem.at[XS], x_recv.at[km], (d, mate)).start()

    def swapped(k):
        @pl.when(jnp.logical_not(native))
        def _():
            @pl.loop(0, 3)
            def _(m):
                wait_bytes(w_buf.at[1 - c, k, m], x_recv.at[3 * k + m])

    def mat(k, m):
        return jnp.concatenate([w_buf[0, k, m], w_buf[1, k, m]], axis=1)

    def hidden_units(k):
        @pl.loop(0, rows // row_block)
        def _(i):
            sl = cols(i, row_block)
            x = x_buf[sl, :]
            gate = dot(x, mat(k, 0))
            up = dot(x, mat(k, 1))
            sigma = jax.nn.sigmoid(gate)
            act = gate * sigma
            hid[k, sl, :] = (act * up).astype(BF16)
            dh = dot(c_buf[sl, :], mat(k, 2))
            dgate[k, sl, :] = (dh * up * (sigma * (1.0 + gate * (1.0 - sigma)))).astype(BF16)
            dup[k, sl, :] = (dh * act).astype(BF16)

    def outer(k):
        @pl.loop(0, width // block)
        def _(i):
            sl = cols(i)
            pair = jnp.concatenate([dgate[k], dup[k]], axis=1)
            both = dot_outer(x_buf[:, sl], pair).astype(BF16)
            down = dot_outer(c_buf[:, sl], hid[k]).astype(BF16)
            dpart[0, k, 0, sl, :] = both[:, :LANES]
            dpart[1, k, 0, sl, :] = both[:, LANES:CHUNK]
            dpart[0, k, 1, sl, :] = both[:, CHUNK : CHUNK + LANES]
            dpart[1, k, 1, sl, :] = both[:, CHUNK + LANES :]
            dpart[0, k, 2, sl, :] = down[:, :LANES]
            dpart[1, k, 2, sl, :] = down[:, LANES:]

        remote(dpart.at[1 - c, k], dx_buf.at[k], one_sem.at[DS], dx_recv.at[k], (d, mate)).start()

    def rows_of(k, m, sl):
        return jnp.concatenate([w_buf[0, k, m, sl, :], w_buf[1, k, m, sl, :]], axis=1)

    def produce():
        @pl.loop(0, width // block)
        def _(i):
            sl = cols(i)
            acc = dot_rows(hid[0], rows_of(0, 2, sl))
            for k in range(1, chunks):
                acc += dot_rows(hid[k], rows_of(k, 2, sl))
            po[:, sl] = acc.astype(BF16)

    def pick_grads():
        @pl.loop(0, width // block)
        def _(i):
            sl = cols(i)
            acc = dot_rows(dgate[0], rows_of(0, 0, sl))
            acc += dot_rows(dup[0], rows_of(0, 1, sl))
            for k in range(1, chunks):
                acc += dot_rows(dgate[k], rows_of(k, 0, sl))
                acc += dot_rows(dup[k], rows_of(k, 1, sl))
            pg[:, sl] = acc.astype(BF16)

    def chain(km):
        k = lax.div(km, 3)
        m = lax.rem(km, 3)

        @pl.when(m == 0)
        def _():
            wait_bytes(dx_buf.at[k], dx_recv.at[k])

        @pl.loop(0, QUARTERS)
        def _(q):
            i = QUARTERS * km + q
            sl = pl.ds(pl.multiple_of(q * quarter, quarter), quarter)
            mine = piece(dpart.at[c], k, m, q)
            there = piece(ch_buf, k, m, q)
            own = dpart[c, k, m, sl, :].astype(F32) + dx_buf[k, m, sl, :].astype(F32)

            @pl.when(r == 1)
            def _():
                dpart[c, k, m, sl, :] = own.astype(BF16)

            @pl.when(r != 1)
            def _():
                wait_bytes(there, ch_recv.at[i])
                dpart[c, k, m, sl, :] = (own + ch_buf[k, m, sl, :].astype(F32)).astype(BF16)

            @pl.when(r != 0)
            def _():
                remote(mine, there, one_sem.at[HS], ch_recv.at[i], (d, nxt)).start()

        @pl.when(r == 0)
        def _():
            def share(t):
                return dpart.at[c, k, m, pl.ds(pl.multiple_of(t * depth, depth), depth)]

            @pl.when(native)
            def _():
                pltpu.make_async_copy(share(d), fg.at[c, k, m], one_sem.at[FL]).start()

            @pl.when(rootmate)
            def _():
                remote(share(d), fg.at[c, k, m], one_sem.at[FS], one_sem.at[FR], (d, d)).start()

            for t in others:
                remote(share(t), fg.at[c, k, m], one_sem.at[FS], one_sem.at[FR], (t, d)).start()

    @pl.loop(0, width // 512)
    def _(i):
        sl = cols(i, 512)
        st[:, sl] = dot(pick_a[...] + pick_b[...], tok_ref[:, sl]).astype(BF16)

    exchange(st, x_buf, TS, TR, TL)

    @pl.loop(0, width // 512)
    def _(i):
        sl = cols(i, 512)
        cot = cot_ref[:, sl].astype(F32)
        sc[:, sl] = (
            dot(pick_a[...], (gain_a * cot).astype(BF16))
            + dot(pick_b[...], (gain_b * cot).astype(BF16))
        ).astype(BF16)

    exchange(sc, c_buf, CS, CR, CL)

    middle = nz // 2
    early = r < middle
    late = jnp.logical_not(early)

    def groups(first, second, third):
        return jnp.where(r == 1, first, jnp.where(r == 2, second, jnp.where(r == 3, third, 0)))

    def sums(start, stop):
        @pl.loop(start, stop)
        def _(km):
            chain(km)

    @pl.loop(0, 6)
    def _(km):
        weights(km)

    @pl.when(early)
    def _():
        @pl.loop(6, 9)
        def _(km):
            weights(km)

    exchanged(x_buf, TR, TL)
    exchanged(c_buf, CR, CL)
    swapped(0)
    hidden_units(0)
    pl.when(late)(lambda: weights(6))
    outer(0)
    pl.when(late)(lambda: weights(7))
    swapped(1)
    hidden_units(1)
    pl.when(late)(lambda: weights(8))
    outer(1)
    sums(0, groups(3, 0, 0))
    swapped(2)
    hidden_units(2)
    sums(groups(3, 0, 0), groups(4, 0, 0))
    produce()
    exchange(po, bo, OS, OR, OL)
    sums(groups(4, 0, 0), groups(5, 2, 1))
    pick_grads()
    exchange(pg, bg, GS, GR, GL)
    sums(groups(5, 2, 1), groups(6, 3, 2))
    outer(2)
    sums(groups(6, 3, 2), 9)

    exchanged(bo, OR, OL)

    @pl.loop(0, width // 512)
    def _(i):
        sl = cols(i, 512)
        got = bo[:, sl]
        out_ref[:, sl] = (
            gain_a * dot_outer(pick_a[...], got) + gain_b * dot_outer(pick_b[...], got)
        ).astype(BF16)

    exchanged(bg, GR, GL)

    @pl.loop(0, width // 512)
    def _(i):
        sl = cols(i, 512)
        got = bg[:, sl]
        ingrad_ref[:, sl] = (
            dot_outer(pick_a[...], got) + dot_outer(pick_b[...], got)
        ).astype(BF16)

    @pl.when(native)
    def _():
        wait_bytes(fg.at[0], one_sem.at[FL])
        wait_bytes(fg.at[0], one_sem.at[FR])
        wait_bytes(dpart.at[0, :, :, pl.ds(0, width - depth)], one_sem.at[FS])

    @pl.when(jnp.logical_not(native))
    def _():
        wait_bytes(fg, one_sem.at[FR])

    @pl.when(rootmate)
    def _():
        wait_bytes(dpart.at[0], one_sem.at[FS])

    for k in range(chunks):
        for h in range(2):
            sl = slice(CHUNK * k + LANES * h, CHUNK * k + LANES * (h + 1))
            gg_ref[0, :, sl] = fg[h, k, 0]
            gu_ref[0, :, sl] = fg[h, k, 1]
            gd_ref[0, :, sl] = fg[h, k, 2]

    for send, buf in ((TS, st), (CS, sc), (OS, po), (GS, pg)):
        wait_bytes(buf.at[pl.ds(0, rows - SLOTS)], one_sem.at[send])

    @pl.when(r <= nz - 2)
    def _():
        wait_bytes(w_buf.at[0], one_sem.at[WS])

    @pl.when(native)
    def _():
        wait_bytes(w_buf.at[0], one_sem.at[PS])

    @pl.when(jnp.logical_not(rootmate))
    def _():
        wait_bytes(w_buf.at[0], one_sem.at[XS])

    @pl.when(r != 0)
    def _():
        wait_bytes(ch_buf, one_sem.at[HS])

    wait_bytes(dx_buf, one_sem.at[DS])


def shards(n, tokens, routes, route_gains, cotangent, w_gate, w_up, w_down):
    width = tokens.shape[1]
    units = w_gate.shape[2]
    chunks = units // CHUNK
    count = tokens.shape[0]
    depth = width // n
    rows = n * SLOTS

    vmem = pl.BlockSpec(memory_space=pltpu.VMEM)
    anywhere = pl.BlockSpec(memory_space=pl.ANY)
    sem = pltpu.SemaphoreType.DMA
    share = jax.ShapeDtypeStruct((1, depth, units), BF16)
    row_out = jax.ShapeDtypeStruct((count, width), BF16)
    landed = pltpu.VMEM((rows, width), BF16)
    acts = pltpu.VMEM((chunks, rows, CHUNK), BF16)
    half = pltpu.VMEM((chunks, 3, width, LANES), BF16)
    halves = pltpu.VMEM((2, chunks, 3, width, LANES), BF16)
    return pl.pallas_call(
        functools.partial(moe_kernel, n, n // 2),
        out_shape=(row_out, row_out, share, share, share),
        in_specs=[vmem] * 4 + [anywhere] * 3,
        out_specs=(vmem,) * 5,
        scratch_shapes=[
            pltpu.VMEM((rows, count), BF16),
            pltpu.VMEM((rows, count), BF16),
            halves,
            landed,
            landed,
            landed,
            landed,
            acts,
            acts,
            acts,
            halves,
            half,
            half,
            landed,
            landed,
            landed,
            landed,
            pltpu.VMEM((2, chunks, 3, depth, LANES), BF16),
            sem((3 * chunks,)),
            sem((3 * chunks * QUARTERS,)),
            sem((3 * chunks,)),
            sem((3 * chunks * QUARTERS,)),
            sem((chunks,)),
            sem((20,)),
        ],
        compiler_params=pltpu.CompilerParams(
            collective_id=0, has_side_effects=True, vmem_limit_bytes=60 * 2**20
        ),
    )(routes.T, route_gains.T, tokens, cotangent, w_gate, w_up, w_down)


def solution(mesh):
    rows = P(("dp", "expert"), None)
    weights = P("expert", None, None)
    shares = P("expert", "dp", None)
    return jax.shard_map(
        functools.partial(shards, mesh.shape["dp"]),
        mesh=mesh,
        in_specs=(rows, rows, rows, rows, weights, weights, weights),
        out_specs=(rows, rows, shares, shares, shares),
        check_vma=False,
    )
```

```python
import functools
import math

import jax
import jax.numpy as jnp
from jax import lax
from jax.experimental import pallas as pl
from jax.experimental.pallas import tpu as pltpu
from jax.sharding import PartitionSpec as P

SLOTS = 32
LANES = 128
CHUNK = 256
QUARTERS = 8
MESH = pl.DeviceIdType.MESH
OFFSETS = (
    (1, 0), (3, 0), (0, 1), (0, 3), (1, 1), (3, 3), (1, 3), (3, 1),
    (2, 0), (0, 2), (2, 2), (2, 1), (1, 2), (2, 3), (3, 2),
)
F32 = jnp.float32
BF16 = jnp.bfloat16


def dot(a, b):
    return jnp.dot(a, b, preferred_element_type=F32)


def dot_rows(a, b):
    return lax.dot_general(a, b, (((1,), (1,)), ((), ())), preferred_element_type=F32)


def dot_outer(a, b):
    return lax.dot_general(a, b, (((0,), (0,)), ((), ())), preferred_element_type=F32)


def moe_kernel(
    n,
    nz,
    routes_ref,
    gains_ref,
    tok_ref,
    cot_ref,
    wg_ref,
    wu_ref,
    wd_ref,
    out_ref,
    ingrad_ref,
    gg_ref,
    gu_ref,
    gd_ref,
    pick_a,
    pick_b,
    w_buf,
    st,
    sc,
    x_buf,
    c_buf,
    hid,
    dgate,
    dup,
    dpart,
    dx_buf,
    ch_buf,
    po,
    pg,
    bo,
    bg,
    fg,
    loc_sem,
    w_recv,
    x_recv,
    ch_recv,
    dx_recv,
    one_sem,
):
    (TS, TR, TL, CS, CR, CL, OS, OR, OL, GS, GR, GL, WS, PS, XS, HS, DS, FS, FR, FL) = range(20)
    width = tok_ref.shape[1]
    chunks = w_buf.shape[1]
    rows = n * SLOTS
    quarter = width // QUARTERS
    depth = width // n
    block = 256
    row_block = min(block, rows)

    d = lax.axis_index("dp")
    ex = lax.axis_index("expert")
    z = lax.div(ex, 2)
    c = lax.rem(ex, 2)
    sgn = 1 - 2 * c
    r = lax.rem(sgn * (z - lax.div(d, 2)) + nz, nz)
    nxt = 2 * lax.rem(z + sgn + nz, nz) + c
    prv = 2 * lax.rem(z - sgn + nz, nz) + c
    mate = ex + sgn
    native = ex == d
    rootmate = mate == d
    side = math.isqrt(n)
    others = [
        lax.rem(lax.div(d, side) + a, side) * side + lax.rem(lax.rem(d, side) + b, side)
        for a, b in OFFSETS
        if a < side and b < side
    ]

    def remote(src, dst, send, recv, dev):
        return pltpu.make_async_remote_copy(
            src_ref=src, dst_ref=dst, send_sem=send, recv_sem=recv, device_id=dev, device_id_type=MESH
        )

    def wait_bytes(ref, sem):
        pltpu.make_async_copy(ref, ref, sem).wait()

    barrier = pltpu.get_barrier_semaphore()

    def greet(dev):
        pl.semaphore_signal(barrier, inc=1, device_id=dev, device_id_type=MESH)

    @pl.loop(1, n)
    def _(j):
        greet((lax.rem(d + j, n), ex))

    greet((d, mate))
    greet((d, nxt))
    greet((d, prv))

    @pl.when(d != ex)
    def _():
        greet((ex, mate))

    @pl.when(rootmate)
    def _():
        @pl.loop(1, n)
        def _(j):
            greet((lax.rem(d + j, n), d))

    @pl.when(native)
    def _():
        for k in range(chunks):
            for m, ref in enumerate((wg_ref, wu_ref, wd_ref)):
                for h in range(2):
                    pltpu.make_async_copy(
                        ref.at[0, :, pl.ds(CHUNK * k + LANES * h, LANES)],
                        w_buf.at[h, k, m],
                        loc_sem.at[3 * k + m],
                    ).start()

    count = tok_ref.shape[0]

    def iota(shape, dim):
        return lax.broadcasted_iota(jnp.int32, shape, dim)

    def ones(mask):
        return jnp.where(mask, 1.0, 0.0).astype(BF16)

    names = [routes_ref[k : k + 1, :] for k in range(2)]
    named = [name == iota((n, count), 0) for name in names]
    square = (count, count)
    before = dot(ones(named[0]) + ones(named[1]), ones(iota(square, 0) < iota(square, 1)))
    for buf, name, match in zip((pick_a, pick_b), names, named):
        place = jnp.sum(jnp.where(match, before, 0.0), axis=0, keepdims=True).astype(jnp.int32)
        buf[...] = ones(iota((rows, count), 0) == name * SLOTS + place)
    gain_a, gain_b = [
        jnp.sum(
            jnp.where(iota(square, 0) == iota(square, 1), gains_ref[k : k + 1, :], 0.0),
            axis=1,
            keepdims=True,
        )
        for k in range(2)
    ]

    pl.semaphore_wait(
        barrier, n + 2 + jnp.where(d != ex, 1, 0) + jnp.where(rootmate, n - 1, 0)
    )

    def slot_rows(i):
        return pl.ds(pl.multiple_of(i * SLOTS, SLOTS), SLOTS)

    def exchange(src, dst, send, recv, own):
        pltpu.make_async_copy(src.at[slot_rows(d)], dst.at[slot_rows(d)], one_sem.at[own]).start()

        for t in others:
            remote(
                src.at[slot_rows(t)], dst.at[slot_rows(d)], one_sem.at[send], one_sem.at[recv], (t, ex)
            ).start()

    def exchanged(dst, recv, own):
        wait_bytes(dst.at[pl.ds(0, SLOTS)], one_sem.at[own])
        wait_bytes(dst.at[pl.ds(0, rows - SLOTS)], one_sem.at[recv])

    def cols(i, size=block):
        return pl.ds(pl.multiple_of(i * size, size), size)

    def piece(buf, k, m, q):
        return buf.at[k, m, pl.ds(pl.multiple_of(q * quarter, quarter), quarter)]

    def weights(km):
        k = lax.div(km, 3)
        m = lax.rem(km, 3)

        @pl.when(native)
        def _():
            wait_bytes(w_buf.at[:, k, m], loc_sem.at[km])

        @pl.loop(0, QUARTERS)
        def _(q):
            i = QUARTERS * km + q
            mine = piece(w_buf.at[c], k, m, q)

            @pl.when(jnp.logical_not(native))
            def _():
                wait_bytes(mine, w_recv.at[i])

            @pl.when(r <= nz - 2)
            def _():
                remote(mine, mine, one_sem.at[WS], w_recv.at[i], (d, nxt)).start()

            @pl.when(native)
            def _():
                other = piece(w_buf.at[1 - c], k, m, q)
                remote(other, other, one_sem.at[PS], w_recv.at[i], (d, mate)).start()

        @pl.when(jnp.logical_not(rootmate))
        def _():
            half = w_buf.at[c, k, m]
            remote(half, half, one_sem.at[XS], x_recv.at[km], (d, mate)).start()

    def swapped(k):
        @pl.when(jnp.logical_not(native))
        def _():
            @pl.loop(0, 3)
            def _(m):
                wait_bytes(w_buf.at[1 - c, k, m], x_recv.at[3 * k + m])

    def mat(k, m):
        return jnp.concatenate([w_buf[0, k, m], w_buf[1, k, m]], axis=1)

    def hidden_units(k):
        @pl.loop(0, rows // row_block)
        def _(i):
            sl = cols(i, row_block)
            x = x_buf[sl, :]
            gate = dot(x, mat(k, 0))
            up = dot(x, mat(k, 1))
            sigma = jax.nn.sigmoid(gate)
            act = gate * sigma
            hid[k, sl, :] = (act * up).astype(BF16)
            dh = dot(c_buf[sl, :], mat(k, 2))
            dgate[k, sl, :] = (dh * up * (sigma * (1.0 + gate * (1.0 - sigma)))).astype(BF16)
            dup[k, sl, :] = (dh * act).astype(BF16)

    def outer(k):
        @pl.loop(0, width // block)
        def _(i):
            sl = cols(i)
            pair = jnp.concatenate([dgate[k], dup[k]], axis=1)
            both = dot_outer(x_buf[:, sl], pair).astype(BF16)
            down = dot_outer(c_buf[:, sl], hid[k]).astype(BF16)
            dpart[0, k, 0, sl, :] = both[:, :LANES]
            dpart[1, k, 0, sl, :] = both[:, LANES:CHUNK]
            dpart[0, k, 1, sl, :] = both[:, CHUNK : CHUNK + LANES]
            dpart[1, k, 1, sl, :] = both[:, CHUNK + LANES :]
            dpart[0, k, 2, sl, :] = down[:, :LANES]
            dpart[1, k, 2, sl, :] = down[:, LANES:]

        for m in range(3):
            remote(
                dpart.at[1 - c, k, m], dx_buf.at[k, m], one_sem.at[DS], dx_recv.at[3 * k + m], (d, mate)
            ).start()

    def rows_of(k, m, sl):
        return jnp.concatenate([w_buf[0, k, m, sl, :], w_buf[1, k, m, sl, :]], axis=1)

    def produce():
        @pl.loop(0, width // block)
        def _(i):
            sl = cols(i)
            acc = dot_rows(hid[0], rows_of(0, 2, sl))
            for k in range(1, chunks):
                acc += dot_rows(hid[k], rows_of(k, 2, sl))
            po[:, sl] = acc.astype(BF16)

    def pick_grads():
        @pl.loop(0, width // block)
        def _(i):
            sl = cols(i)
            acc = dot_rows(dgate[0], rows_of(0, 0, sl))
            acc += dot_rows(dup[0], rows_of(0, 1, sl))
            for k in range(1, chunks):
                acc += dot_rows(dgate[k], rows_of(k, 0, sl))
                acc += dot_rows(dup[k], rows_of(k, 1, sl))
            pg[:, sl] = acc.astype(BF16)

    def chain(km):
        k = lax.div(km, 3)
        m = lax.rem(km, 3)

        wait_bytes(dx_buf.at[k, m], dx_recv.at[km])

        @pl.loop(0, QUARTERS)
        def _(q):
            i = QUARTERS * km + q
            sl = pl.ds(pl.multiple_of(q * quarter, quarter), quarter)
            mine = piece(dpart.at[c], k, m, q)
            there = piece(ch_buf, k, m, q)
            own = dpart[c, k, m, sl, :].astype(F32) + dx_buf[k, m, sl, :].astype(F32)

            @pl.when(r == 1)
            def _():
                dpart[c, k, m, sl, :] = own.astype(BF16)

            @pl.when(r != 1)
            def _():
                wait_bytes(there, ch_recv.at[i])
                dpart[c, k, m, sl, :] = (own + ch_buf[k, m, sl, :].astype(F32)).astype(BF16)

            @pl.when(r != 0)
            def _():
                remote(mine, there, one_sem.at[HS], ch_recv.at[i], (d, nxt)).start()

        @pl.when(r == 0)
        def _():
            def share(t):
                return dpart.at[c, k, m, pl.ds(pl.multiple_of(t * depth, depth), depth)]

            @pl.when(native)
            def _():
                pltpu.make_async_copy(share(d), fg.at[c, k, m], one_sem.at[FL]).start()

            @pl.when(rootmate)
            def _():
                remote(share(d), fg.at[c, k, m], one_sem.at[FS], one_sem.at[FR], (d, d)).start()

            for t in others:
                remote(share(t), fg.at[c, k, m], one_sem.at[FS], one_sem.at[FR], (t, d)).start()

    @pl.loop(0, width // 512)
    def _(i):
        sl = cols(i, 512)
        st[:, sl] = dot(pick_a[...] + pick_b[...], tok_ref[:, sl]).astype(BF16)

    exchange(st, x_buf, TS, TR, TL)

    @pl.loop(0, width // 512)
    def _(i):
        sl = cols(i, 512)
        cot = cot_ref[:, sl].astype(F32)
        sc[:, sl] = (
            dot(pick_a[...], (gain_a * cot).astype(BF16))
            + dot(pick_b[...], (gain_b * cot).astype(BF16))
        ).astype(BF16)

    exchange(sc, c_buf, CS, CR, CL)

    middle = nz // 2
    early = r < middle
    late = jnp.logical_not(early)

    def groups(first, second, third):
        return jnp.where(r == 1, first, jnp.where(r == 2, second, jnp.where(r == 3, third, 0)))

    def sums(start, stop):
        @pl.loop(start, stop)
        def _(km):
            chain(km)

    @pl.loop(0, 6)
    def _(km):
        weights(km)

    @pl.when(early)
    def _():
        @pl.loop(6, 9)
        def _(km):
            weights(km)

    exchanged(x_buf, TR, TL)
    exchanged(c_buf, CR, CL)
    swapped(0)
    hidden_units(0)
    pl.when(late)(lambda: weights(6))
    outer(0)
    pl.when(late)(lambda: weights(7))
    swapped(1)
    hidden_units(1)
    pl.when(late)(lambda: weights(8))
    outer(1)
    sums(0, groups(3, 0, 0))
    swapped(2)
    hidden_units(2)
    sums(groups(3, 0, 0), groups(4, 0, 0))
    produce()
    exchange(po, bo, OS, OR, OL)
    sums(groups(4, 0, 0), groups(5, 2, 1))
    pick_grads()
    exchange(pg, bg, GS, GR, GL)
    sums(groups(5, 2, 1), groups(6, 3, 2))
    outer(2)
    sums(groups(6, 3, 2), 9)

    exchanged(bo, OR, OL)

    @pl.loop(0, width // 512)
    def _(i):
        sl = cols(i, 512)
        got = bo[:, sl]
        out_ref[:, sl] = (
            gain_a * dot_outer(pick_a[...], got) + gain_b * dot_outer(pick_b[...], got)
        ).astype(BF16)

    exchanged(bg, GR, GL)

    @pl.loop(0, width // 512)
    def _(i):
        sl = cols(i, 512)
        got = bg[:, sl]
        ingrad_ref[:, sl] = (
            dot_outer(pick_a[...], got) + dot_outer(pick_b[...], got)
        ).astype(BF16)

    @pl.when(native)
    def _():
        wait_bytes(fg.at[0], one_sem.at[FL])
        wait_bytes(fg.at[0], one_sem.at[FR])
        wait_bytes(dpart.at[0, :, :, pl.ds(0, width - depth)], one_sem.at[FS])

    @pl.when(jnp.logical_not(native))
    def _():
        wait_bytes(fg, one_sem.at[FR])

    @pl.when(rootmate)
    def _():
        wait_bytes(dpart.at[0], one_sem.at[FS])

    for k in range(chunks):
        for h in range(2):
            sl = slice(CHUNK * k + LANES * h, CHUNK * k + LANES * (h + 1))
            gg_ref[0, :, sl] = fg[h, k, 0]
            gu_ref[0, :, sl] = fg[h, k, 1]
            gd_ref[0, :, sl] = fg[h, k, 2]

    for send, buf in ((TS, st), (CS, sc), (OS, po), (GS, pg)):
        wait_bytes(buf.at[pl.ds(0, rows - SLOTS)], one_sem.at[send])

    @pl.when(r <= nz - 2)
    def _():
        wait_bytes(w_buf.at[0], one_sem.at[WS])

    @pl.when(native)
    def _():
        wait_bytes(w_buf.at[0], one_sem.at[PS])

    @pl.when(jnp.logical_not(rootmate))
    def _():
        wait_bytes(w_buf.at[0], one_sem.at[XS])

    @pl.when(r != 0)
    def _():
        wait_bytes(ch_buf, one_sem.at[HS])

    wait_bytes(dx_buf, one_sem.at[DS])


def hand_over(*refs):
    sems = refs[10]
    copies = [pltpu.make_async_copy(refs[i], refs[5 + i], sems.at[i]) for i in range(5)]
    for copy in copies:
        copy.start()
    for copy in copies:
        copy.wait()


def shards(n, tokens, routes, route_gains, cotangent, w_gate, w_up, w_down):
    width = tokens.shape[1]
    units = w_gate.shape[2]
    chunks = units // CHUNK
    count = tokens.shape[0]
    depth = width // n
    rows = n * SLOTS

    vmem = pl.BlockSpec(memory_space=pltpu.VMEM)
    anywhere = pl.BlockSpec(memory_space=pl.ANY)
    sem = pltpu.SemaphoreType.DMA
    share = jax.ShapeDtypeStruct((1, depth, units), BF16)
    row_out = jax.ShapeDtypeStruct((count, width), BF16)
    landed = pltpu.VMEM((rows, width), BF16)
    acts = pltpu.VMEM((chunks, rows, CHUNK), BF16)
    half = pltpu.VMEM((chunks, 3, width, LANES), BF16)
    halves = pltpu.VMEM((2, chunks, 3, width, LANES), BF16)
    results = pl.pallas_call(
        functools.partial(moe_kernel, n, n // 2),
        out_shape=(row_out, row_out, share, share, share),
        in_specs=[vmem] * 4 + [anywhere] * 3,
        out_specs=(vmem,) * 5,
        scratch_shapes=[
            pltpu.VMEM((rows, count), BF16),
            pltpu.VMEM((rows, count), BF16),
            halves,
            landed,
            landed,
            landed,
            landed,
            acts,
            acts,
            acts,
            halves,
            half,
            half,
            landed,
            landed,
            landed,
            landed,
            pltpu.VMEM((2, chunks, 3, depth, LANES), BF16),
            sem((3 * chunks,)),
            sem((3 * chunks * QUARTERS,)),
            sem((3 * chunks,)),
            sem((3 * chunks * QUARTERS,)),
            sem((3 * chunks,)),
            sem((20,)),
        ],
        compiler_params=pltpu.CompilerParams(
            collective_id=0, has_side_effects=True, vmem_limit_bytes=60 * 2**20
        ),
    )(routes.T, route_gains.T, tokens, cotangent, w_gate, w_up, w_down)
    return pl.pallas_call(
        hand_over,
        out_shape=(row_out, row_out, share, share, share),
        in_specs=[anywhere] * 5,
        out_specs=(anywhere,) * 5,
        scratch_shapes=[sem((5,))],
    )(*results)


def solution(mesh):
    rows = P(("dp", "expert"), None)
    weights = P("expert", None, None)
    shares = P("expert", "dp", None)
    return jax.shard_map(
        functools.partial(shards, mesh.shape["dp"]),
        mesh=mesh,
        in_specs=(rows, rows, rows, rows, weights, weights, weights),
        out_specs=(rows, rows, shares, shares, shares),
        check_vma=False,
    )
```

```python
import functools
import math

import jax
import jax.numpy as jnp
from jax import lax
from jax.experimental import pallas as pl
from jax.experimental.pallas import tpu as pltpu
from jax.sharding import PartitionSpec as P

SLOTS = 32
LANES = 128
CHUNK = 256
QUARTERS = 8
AHEAD = 4
SUMS_AHEAD = 24
MESH = pl.DeviceIdType.MESH
OFFSETS = (
    (1, 0), (3, 0), (0, 1), (0, 3), (1, 1), (3, 3), (1, 3), (3, 1),
    (2, 0), (0, 2), (2, 2), (2, 1), (1, 2), (2, 3), (3, 2),
)
F32 = jnp.float32
BF16 = jnp.bfloat16


def dot(a, b):
    return jnp.dot(a, b, preferred_element_type=F32)


def dot_rows(a, b):
    return lax.dot_general(a, b, (((1,), (1,)), ((), ())), preferred_element_type=F32)


def dot_outer(a, b):
    return lax.dot_general(a, b, (((0,), (0,)), ((), ())), preferred_element_type=F32)


def moe_kernel(
    n,
    nz,
    routes_ref,
    gains_ref,
    tok_ref,
    cot_ref,
    wg_ref,
    wu_ref,
    wd_ref,
    out_ref,
    ingrad_ref,
    gg_ref,
    gu_ref,
    gd_ref,
    pick_a,
    pick_b,
    w_buf,
    st,
    sc,
    x_buf,
    c_buf,
    hid,
    dgate,
    dup,
    dpart,
    dx_buf,
    ch_buf,
    po,
    pg,
    bo,
    bg,
    fg,
    loc_sem,
    w_recv,
    x_recv,
    ch_recv,
    dx_recv,
    w_send,
    ch_send,
    one_sem,
):
    (TS, TR, TL, CS, CR, CL, OS, OR, OL, GS, GR, GL, WS, PS, XS, HS, DS, FS, FR, FL) = range(20)
    width = tok_ref.shape[1]
    chunks = w_buf.shape[1]
    rows = n * SLOTS
    quarter = width // QUARTERS
    depth = width // n
    block = 256
    row_block = min(block, rows)

    d = lax.axis_index("dp")
    ex = lax.axis_index("expert")
    z = lax.div(ex, 2)
    c = lax.rem(ex, 2)
    sgn = 1 - 2 * c
    r = lax.rem(sgn * (z - lax.div(d, 2)) + nz, nz)
    nxt = 2 * lax.rem(z + sgn + nz, nz) + c
    prv = 2 * lax.rem(z - sgn + nz, nz) + c
    mate = ex + sgn
    native = ex == d
    rootmate = mate == d
    side = math.isqrt(n)
    others = [
        lax.rem(lax.div(d, side) + a, side) * side + lax.rem(lax.rem(d, side) + b, side)
        for a, b in OFFSETS
        if a < side and b < side
    ]

    def remote(src, dst, send, recv, dev):
        return pltpu.make_async_remote_copy(
            src_ref=src, dst_ref=dst, send_sem=send, recv_sem=recv, device_id=dev, device_id_type=MESH
        )

    def wait_bytes(ref, sem):
        pltpu.make_async_copy(ref, ref, sem).wait()

    barrier = pltpu.get_barrier_semaphore()

    def greet(dev):
        pl.semaphore_signal(barrier, inc=1, device_id=dev, device_id_type=MESH)

    @pl.loop(1, n)
    def _(j):
        greet((lax.rem(d + j, n), ex))

    greet((d, mate))
    greet((d, nxt))
    greet((d, prv))

    @pl.when(d != ex)
    def _():
        greet((ex, mate))

    @pl.when(rootmate)
    def _():
        @pl.loop(1, n)
        def _(j):
            greet((lax.rem(d + j, n), d))

    @pl.when(native)
    def _():
        for k in range(chunks):
            for m, ref in enumerate((wg_ref, wu_ref, wd_ref)):
                for h in range(2):
                    pltpu.make_async_copy(
                        ref.at[0, :, pl.ds(CHUNK * k + LANES * h, LANES)],
                        w_buf.at[h, k, m],
                        loc_sem.at[3 * k + m],
                    ).start()

    count = tok_ref.shape[0]

    def iota(shape, dim):
        return lax.broadcasted_iota(jnp.int32, shape, dim)

    def ones(mask):
        return jnp.where(mask, 1.0, 0.0).astype(BF16)

    names = [routes_ref[k : k + 1, :] for k in range(2)]
    named = [name == iota((n, count), 0) for name in names]
    square = (count, count)
    before = dot(ones(named[0]) + ones(named[1]), ones(iota(square, 0) < iota(square, 1)))
    for buf, name, match in zip((pick_a, pick_b), names, named):
        place = jnp.sum(jnp.where(match, before, 0.0), axis=0, keepdims=True).astype(jnp.int32)
        buf[...] = ones(iota((rows, count), 0) == name * SLOTS + place)
    gain_a, gain_b = [
        jnp.sum(
            jnp.where(iota(square, 0) == iota(square, 1), gains_ref[k : k + 1, :], 0.0),
            axis=1,
            keepdims=True,
        )
        for k in range(2)
    ]

    pl.semaphore_wait(
        barrier, n + 2 + jnp.where(d != ex, 1, 0) + jnp.where(rootmate, n - 1, 0)
    )

    def slot_rows(i):
        return pl.ds(pl.multiple_of(i * SLOTS, SLOTS), SLOTS)

    def exchange(src, dst, send, recv, own):
        pltpu.make_async_copy(src.at[slot_rows(d)], dst.at[slot_rows(d)], one_sem.at[own]).start()

        for t in others:
            remote(
                src.at[slot_rows(t)], dst.at[slot_rows(d)], one_sem.at[send], one_sem.at[recv], (t, ex)
            ).start()

    def exchanged(dst, recv, own):
        wait_bytes(dst.at[pl.ds(0, SLOTS)], one_sem.at[own])
        wait_bytes(dst.at[pl.ds(0, rows - SLOTS)], one_sem.at[recv])

    def cols(i, size=block):
        return pl.ds(pl.multiple_of(i * size, size), size)

    def piece(buf, k, m, q):
        return buf.at[k, m, pl.ds(pl.multiple_of(q * quarter, quarter), quarter)]

    def weights(km):
        k = lax.div(km, 3)
        m = lax.rem(km, 3)

        @pl.when(native)
        def _():
            wait_bytes(w_buf.at[:, k, m], loc_sem.at[km])

        @pl.loop(0, QUARTERS)
        def _(q):
            i = QUARTERS * km + q
            mine = piece(w_buf.at[c], k, m, q)

            @pl.when(jnp.logical_not(native))
            def _():
                wait_bytes(mine, w_recv.at[i])

            @pl.when(r <= nz - 2)
            def _():
                slot = w_send.at[lax.rem(i, AHEAD)]

                @pl.when(i >= AHEAD)
                def _():
                    wait_bytes(mine, slot)

                remote(mine, mine, slot, w_recv.at[i], (d, nxt)).start()

            @pl.when(native)
            def _():
                other = piece(w_buf.at[1 - c], k, m, q)
                remote(other, other, one_sem.at[PS], w_recv.at[i], (d, mate)).start()

        @pl.when(jnp.logical_not(rootmate))
        def _():
            half = w_buf.at[c, k, m]
            remote(half, half, one_sem.at[XS], x_recv.at[km], (d, mate)).start()

    def swapped(k):
        @pl.when(jnp.logical_not(native))
        def _():
            @pl.loop(0, 3)
            def _(m):
                wait_bytes(w_buf.at[1 - c, k, m], x_recv.at[3 * k + m])

    def mat(k, m):
        return jnp.concatenate([w_buf[0, k, m], w_buf[1, k, m]], axis=1)

    def hidden_units(k):
        @pl.loop(0, rows // row_block)
        def _(i):
            sl = cols(i, row_block)
            x = x_buf[sl, :]
            gate = dot(x, mat(k, 0))
            up = dot(x, mat(k, 1))
            sigma = jax.nn.sigmoid(gate)
            act = gate * sigma
            hid[k, sl, :] = (act * up).astype(BF16)
            dh = dot(c_buf[sl, :], mat(k, 2))
            dgate[k, sl, :] = (dh * up * (sigma * (1.0 + gate * (1.0 - sigma)))).astype(BF16)
            dup[k, sl, :] = (dh * act).astype(BF16)

    def outer(k):
        @pl.loop(0, width // block)
        def _(i):
            sl = cols(i)
            pair = jnp.concatenate([dgate[k], dup[k]], axis=1)
            both = dot_outer(x_buf[:, sl], pair).astype(BF16)
            down = dot_outer(c_buf[:, sl], hid[k]).astype(BF16)
            dpart[0, k, 0, sl, :] = both[:, :LANES]
            dpart[1, k, 0, sl, :] = both[:, LANES:CHUNK]
            dpart[0, k, 1, sl, :] = both[:, CHUNK : CHUNK + LANES]
            dpart[1, k, 1, sl, :] = both[:, CHUNK + LANES :]
            dpart[0, k, 2, sl, :] = down[:, :LANES]
            dpart[1, k, 2, sl, :] = down[:, LANES:]

        for m in range(3):
            remote(
                dpart.at[1 - c, k, m], dx_buf.at[k, m], one_sem.at[DS], dx_recv.at[3 * k + m], (d, mate)
            ).start()

    def rows_of(k, m, sl):
        return jnp.concatenate([w_buf[0, k, m, sl, :], w_buf[1, k, m, sl, :]], axis=1)

    def produce():
        @pl.loop(0, width // block)
        def _(i):
            sl = cols(i)
            acc = dot_rows(hid[0], rows_of(0, 2, sl))
            for k in range(1, chunks):
                acc += dot_rows(hid[k], rows_of(k, 2, sl))
            po[:, sl] = acc.astype(BF16)

    def pick_grads():
        @pl.loop(0, width // block)
        def _(i):
            sl = cols(i)
            acc = dot_rows(dgate[0], rows_of(0, 0, sl))
            acc += dot_rows(dup[0], rows_of(0, 1, sl))
            for k in range(1, chunks):
                acc += dot_rows(dgate[k], rows_of(k, 0, sl))
                acc += dot_rows(dup[k], rows_of(k, 1, sl))
            pg[:, sl] = acc.astype(BF16)

    def chain(km):
        k = lax.div(km, 3)
        m = lax.rem(km, 3)

        wait_bytes(dx_buf.at[k, m], dx_recv.at[km])

        @pl.loop(0, QUARTERS)
        def _(q):
            i = QUARTERS * km + q
            sl = pl.ds(pl.multiple_of(q * quarter, quarter), quarter)
            mine = piece(dpart.at[c], k, m, q)
            there = piece(ch_buf, k, m, q)
            own = dpart[c, k, m, sl, :].astype(F32) + dx_buf[k, m, sl, :].astype(F32)

            @pl.when(r == 1)
            def _():
                dpart[c, k, m, sl, :] = own.astype(BF16)

            @pl.when(r != 1)
            def _():
                wait_bytes(there, ch_recv.at[i])
                dpart[c, k, m, sl, :] = (own + ch_buf[k, m, sl, :].astype(F32)).astype(BF16)

            @pl.when(r != 0)
            def _():
                slot = ch_send.at[lax.rem(i, SUMS_AHEAD)]

                @pl.when(i >= SUMS_AHEAD)
                def _():
                    wait_bytes(mine, slot)

                remote(mine, there, slot, ch_recv.at[i], (d, nxt)).start()

        @pl.when(r == 0)
        def _():
            def share(t):
                return dpart.at[c, k, m, pl.ds(pl.multiple_of(t * depth, depth), depth)]

            @pl.when(native)
            def _():
                pltpu.make_async_copy(share(d), fg.at[c, k, m], one_sem.at[FL]).start()

            @pl.when(rootmate)
            def _():
                remote(share(d), fg.at[c, k, m], one_sem.at[FS], one_sem.at[FR], (d, d)).start()

            for t in others:
                remote(share(t), fg.at[c, k, m], one_sem.at[FS], one_sem.at[FR], (t, d)).start()

    @pl.loop(0, width // 512)
    def _(i):
        sl = cols(i, 512)
        st[:, sl] = dot(pick_a[...] + pick_b[...], tok_ref[:, sl]).astype(BF16)

    exchange(st, x_buf, TS, TR, TL)

    @pl.loop(0, width // 512)
    def _(i):
        sl = cols(i, 512)
        cot = cot_ref[:, sl].astype(F32)
        sc[:, sl] = (
            dot(pick_a[...], (gain_a * cot).astype(BF16))
            + dot(pick_b[...], (gain_b * cot).astype(BF16))
        ).astype(BF16)

    exchange(sc, c_buf, CS, CR, CL)

    middle = nz // 2
    early = r < middle
    late = jnp.logical_not(early)

    def groups(first, second, third):
        return jnp.where(r == 1, first, jnp.where(r == 2, second, jnp.where(r == 3, third, 0)))

    def sums(start, stop):
        @pl.loop(start, stop)
        def _(km):
            chain(km)

    @pl.loop(0, 6)
    def _(km):
        weights(km)

    @pl.when(early)
    def _():
        @pl.loop(6, 9)
        def _(km):
            weights(km)

    exchanged(x_buf, TR, TL)
    exchanged(c_buf, CR, CL)
    swapped(0)
    hidden_units(0)
    pl.when(late)(lambda: weights(6))
    outer(0)
    pl.when(late)(lambda: weights(7))
    swapped(1)
    hidden_units(1)
    pl.when(late)(lambda: weights(8))
    outer(1)
    sums(0, groups(3, 0, 0))
    swapped(2)
    hidden_units(2)
    sums(groups(3, 0, 0), groups(4, 0, 0))
    produce()
    exchange(po, bo, OS, OR, OL)
    sums(groups(4, 0, 0), groups(5, 2, 1))
    pick_grads()
    exchange(pg, bg, GS, GR, GL)
    sums(groups(5, 2, 1), groups(6, 3, 2))
    outer(2)
    sums(groups(6, 3, 2), 9)

    exchanged(bo, OR, OL)

    @pl.loop(0, width // 512)
    def _(i):
        sl = cols(i, 512)
        got = bo[:, sl]
        out_ref[:, sl] = (
            gain_a * dot_outer(pick_a[...], got) + gain_b * dot_outer(pick_b[...], got)
        ).astype(BF16)

    exchanged(bg, GR, GL)

    @pl.loop(0, width // 512)
    def _(i):
        sl = cols(i, 512)
        got = bg[:, sl]
        ingrad_ref[:, sl] = (
            dot_outer(pick_a[...], got) + dot_outer(pick_b[...], got)
        ).astype(BF16)

    @pl.when(native)
    def _():
        wait_bytes(fg.at[0], one_sem.at[FL])
        wait_bytes(fg.at[0], one_sem.at[FR])
        wait_bytes(dpart.at[0, :, :, pl.ds(0, width - depth)], one_sem.at[FS])

    @pl.when(jnp.logical_not(native))
    def _():
        wait_bytes(fg, one_sem.at[FR])

    @pl.when(rootmate)
    def _():
        wait_bytes(dpart.at[0], one_sem.at[FS])

    for k in range(chunks):
        for h in range(2):
            sl = slice(CHUNK * k + LANES * h, CHUNK * k + LANES * (h + 1))
            gg_ref[0, :, sl] = fg[h, k, 0]
            gu_ref[0, :, sl] = fg[h, k, 1]
            gd_ref[0, :, sl] = fg[h, k, 2]

    for send, buf in ((TS, st), (CS, sc), (OS, po), (GS, pg)):
        wait_bytes(buf.at[pl.ds(0, rows - SLOTS)], one_sem.at[send])

    @pl.when(r <= nz - 2)
    def _():
        @pl.loop(0, AHEAD)
        def _(i):
            wait_bytes(w_buf.at[0, 0, 0, pl.ds(0, quarter)], w_send.at[i])

    @pl.when(native)
    def _():
        wait_bytes(w_buf.at[0], one_sem.at[PS])

    @pl.when(jnp.logical_not(rootmate))
    def _():
        wait_bytes(w_buf.at[0], one_sem.at[XS])

    @pl.when(r != 0)
    def _():
        @pl.loop(0, SUMS_AHEAD)
        def _(i):
            wait_bytes(ch_buf.at[0, 0, pl.ds(0, quarter)], ch_send.at[i])

    wait_bytes(dx_buf, one_sem.at[DS])


def hand_over(*refs):
    for i in range(5):
        refs[5 + i][...] = refs[i][...]


def shards(n, tokens, routes, route_gains, cotangent, w_gate, w_up, w_down):
    width = tokens.shape[1]
    units = w_gate.shape[2]
    chunks = units // CHUNK
    count = tokens.shape[0]
    depth = width // n
    rows = n * SLOTS

    vmem = pl.BlockSpec(memory_space=pltpu.VMEM)
    anywhere = pl.BlockSpec(memory_space=pl.ANY)
    sem = pltpu.SemaphoreType.DMA
    share = jax.ShapeDtypeStruct((1, depth, units), BF16)
    row_out = jax.ShapeDtypeStruct((count, width), BF16)
    landed = pltpu.VMEM((rows, width), BF16)
    acts = pltpu.VMEM((chunks, rows, CHUNK), BF16)
    half = pltpu.VMEM((chunks, 3, width, LANES), BF16)
    halves = pltpu.VMEM((2, chunks, 3, width, LANES), BF16)
    results = pl.pallas_call(
        functools.partial(moe_kernel, n, n // 2),
        out_shape=(row_out, row_out, share, share, share),
        in_specs=[vmem] * 4 + [anywhere] * 3,
        out_specs=(vmem,) * 5,
        scratch_shapes=[
            pltpu.VMEM((rows, count), BF16),
            pltpu.VMEM((rows, count), BF16),
            halves,
            landed,
            landed,
            landed,
            landed,
            acts,
            acts,
            acts,
            halves,
            half,
            half,
            landed,
            landed,
            landed,
            landed,
            pltpu.VMEM((2, chunks, 3, depth, LANES), BF16),
            sem((3 * chunks,)),
            sem((3 * chunks * QUARTERS,)),
            sem((3 * chunks,)),
            sem((3 * chunks * QUARTERS,)),
            sem((3 * chunks,)),
            sem((AHEAD,)),
            sem((SUMS_AHEAD,)),
            sem((20,)),
        ],
        compiler_params=pltpu.CompilerParams(
            collective_id=0, has_side_effects=True, vmem_limit_bytes=60 * 2**20
        ),
    )(routes.T, route_gains.T, tokens, cotangent, w_gate, w_up, w_down)
    return pl.pallas_call(
        hand_over,
        out_shape=(row_out, row_out, share, share, share),
        in_specs=[vmem] * 5,
        out_specs=(vmem,) * 5,
    )(*results)


def solution(mesh):
    rows = P(("dp", "expert"), None)
    weights = P("expert", None, None)
    shares = P("expert", "dp", None)
    return jax.shard_map(
        functools.partial(shards, mesh.shape["dp"]),
        mesh=mesh,
        in_specs=(rows, rows, rows, rows, weights, weights, weights),
        out_specs=(rows, rows, shares, shares, shares),
        check_vma=False,
    )
```

```python
import functools
import math

import jax
import jax.numpy as jnp
from jax import lax
from jax.experimental import pallas as pl
from jax.experimental.pallas import tpu as pltpu
from jax.sharding import PartitionSpec as P

SLOTS = 32
LANES = 128
CHUNK = 256
QUARTERS = 8
MESH = pl.DeviceIdType.MESH
OFFSETS = (
    (1, 0), (3, 0), (0, 1), (0, 3), (1, 1), (3, 3), (1, 3), (3, 1),
    (2, 0), (0, 2), (2, 2), (2, 1), (1, 2), (2, 3), (3, 2),
)
F32 = jnp.float32
BF16 = jnp.bfloat16


def dot(a, b):
    return jnp.dot(a, b, preferred_element_type=F32)


def dot_rows(a, b):
    return lax.dot_general(a, b, (((1,), (1,)), ((), ())), preferred_element_type=F32)


def dot_outer(a, b):
    return lax.dot_general(a, b, (((0,), (0,)), ((), ())), preferred_element_type=F32)


def moe_kernel(
    n,
    nz,
    routes_ref,
    gains_ref,
    tok_ref,
    cot_ref,
    wg_ref,
    wu_ref,
    wd_ref,
    out_ref,
    ingrad_ref,
    gg_ref,
    gu_ref,
    gd_ref,
    pick_a,
    pick_b,
    w_buf,
    st,
    sc,
    x_buf,
    c_buf,
    hid,
    dgate,
    dup,
    dpart,
    dx_buf,
    ch_buf,
    po,
    pg,
    bo,
    bg,
    fg,
    loc_sem,
    w_recv,
    x_recv,
    ch_recv,
    dx_recv,
    one_sem,
):
    (TS, TR, TL, CS, CR, CL, OS, OR, OL, GS, GR, GL, WS, PS, XS, HS, DS, FS, FR, FL) = range(20)
    width = tok_ref.shape[1]
    chunks = w_buf.shape[1]
    rows = n * SLOTS
    quarter = width // QUARTERS
    depth = width // n
    block = 256
    row_block = min(block, rows)

    d = lax.axis_index("dp")
    ex = lax.axis_index("expert")
    z = lax.div(ex, 2)
    c = lax.rem(ex, 2)
    sgn = 1 - 2 * c
    r = lax.rem(sgn * (z - lax.div(d, 2)) + nz, nz)
    nxt = 2 * lax.rem(z + sgn + nz, nz) + c
    prv = 2 * lax.rem(z - sgn + nz, nz) + c
    mate = ex + sgn
    native = ex == d
    rootmate = mate == d
    side = math.isqrt(n)
    others = [
        lax.rem(lax.div(d, side) + a, side) * side + lax.rem(lax.rem(d, side) + b, side)
        for a, b in OFFSETS
        if a < side and b < side
    ]

    def remote(src, dst, send, recv, dev):
        return pltpu.make_async_remote_copy(
            src_ref=src, dst_ref=dst, send_sem=send, recv_sem=recv, device_id=dev, device_id_type=MESH
        )

    def wait_bytes(ref, sem):
        pltpu.make_async_copy(ref, ref, sem).wait()

    barrier = pltpu.get_barrier_semaphore()

    def greet(dev):
        pl.semaphore_signal(barrier, inc=1, device_id=dev, device_id_type=MESH)

    @pl.loop(1, n)
    def _(j):
        greet((lax.rem(d + j, n), ex))

    greet((d, mate))
    greet((d, nxt))
    greet((d, prv))

    @pl.when(d != ex)
    def _():
        greet((ex, mate))

    @pl.when(rootmate)
    def _():
        @pl.loop(1, n)
        def _(j):
            greet((lax.rem(d + j, n), d))

    @pl.when(native)
    def _():
        for k in range(chunks):
            for m, ref in enumerate((wg_ref, wu_ref, wd_ref)):
                for h in range(2):
                    pltpu.make_async_copy(
                        ref.at[0, :, pl.ds(CHUNK * k + LANES * h, LANES)],
                        w_buf.at[h, k, m],
                        loc_sem.at[3 * k + m],
                    ).start()

    count = tok_ref.shape[0]

    def iota(shape, dim):
        return lax.broadcasted_iota(jnp.int32, shape, dim)

    def ones(mask):
        return jnp.where(mask, 1.0, 0.0).astype(BF16)

    names = [routes_ref[k : k + 1, :] for k in range(2)]
    named = [name == iota((n, count), 0) for name in names]
    square = (count, count)
    before = dot(ones(named[0]) + ones(named[1]), ones(iota(square, 0) < iota(square, 1)))
    for buf, name, match in zip((pick_a, pick_b), names, named):
        place = jnp.sum(jnp.where(match, before, 0.0), axis=0, keepdims=True).astype(jnp.int32)
        buf[...] = ones(iota((rows, count), 0) == name * SLOTS + place)
    gain_a, gain_b = [
        jnp.sum(
            jnp.where(iota(square, 0) == iota(square, 1), gains_ref[k : k + 1, :], 0.0),
            axis=1,
            keepdims=True,
        )
        for k in range(2)
    ]

    pl.semaphore_wait(
        barrier, n + 2 + jnp.where(d != ex, 1, 0) + jnp.where(rootmate, n - 1, 0)
    )

    def slot_rows(i):
        return pl.ds(pl.multiple_of(i * SLOTS, SLOTS), SLOTS)

    def exchange(src, dst, send, recv, own):
        pltpu.make_async_copy(src.at[slot_rows(d)], dst.at[slot_rows(d)], one_sem.at[own]).start()

        for t in others:
            remote(
                src.at[slot_rows(t)], dst.at[slot_rows(d)], one_sem.at[send], one_sem.at[recv], (t, ex)
            ).start()

    def exchanged(dst, recv, own):
        wait_bytes(dst.at[pl.ds(0, SLOTS)], one_sem.at[own])
        wait_bytes(dst.at[pl.ds(0, rows - SLOTS)], one_sem.at[recv])

    def cols(i, size=block):
        return pl.ds(pl.multiple_of(i * size, size), size)

    def piece(buf, k, m, q):
        return buf.at[k, m, pl.ds(pl.multiple_of(q * quarter, quarter), quarter)]

    def weights(km):
        k = lax.div(km, 3)
        m = lax.rem(km, 3)

        @pl.when(native)
        def _():
            wait_bytes(w_buf.at[:, k, m], loc_sem.at[km])

        @pl.loop(0, QUARTERS)
        def _(q):
            i = QUARTERS * km + q
            mine = piece(w_buf.at[c], k, m, q)

            @pl.when(jnp.logical_not(native))
            def _():
                wait_bytes(mine, w_recv.at[i])

            @pl.when(r <= nz - 2)
            def _():
                remote(mine, mine, one_sem.at[WS], w_recv.at[i], (d, nxt)).start()

            @pl.when(native)
            def _():
                other = piece(w_buf.at[1 - c], k, m, q)
                remote(other, other, one_sem.at[PS], w_recv.at[i], (d, mate)).start()

        @pl.when(jnp.logical_not(rootmate))
        def _():
            half = w_buf.at[c, k, m]
            remote(half, half, one_sem.at[XS], x_recv.at[km], (d, mate)).start()

    def swapped(k):
        @pl.when(jnp.logical_not(native))
        def _():
            @pl.loop(0, 3)
            def _(m):
                wait_bytes(w_buf.at[1 - c, k, m], x_recv.at[3 * k + m])

    def mat(k, m):
        return jnp.concatenate([w_buf[0, k, m], w_buf[1, k, m]], axis=1)

    def hidden_units(k):
        @pl.loop(0, rows // row_block)
        def _(i):
            sl = cols(i, row_block)
            x = x_buf[sl, :]
            gate = dot(x, mat(k, 0))
            up = dot(x, mat(k, 1))
            sigma = jax.nn.sigmoid(gate)
            act = gate * sigma
            hid[k, sl, :] = (act * up).astype(BF16)
            dh = dot(c_buf[sl, :], mat(k, 2))
            dgate[k, sl, :] = (dh * up * (sigma * (1.0 + gate * (1.0 - sigma)))).astype(BF16)
            dup[k, sl, :] = (dh * act).astype(BF16)

    def outer(k):
        @pl.loop(0, width // block)
        def _(i):
            sl = cols(i)
            pair = jnp.concatenate([dgate[k], dup[k]], axis=1)
            both = dot_outer(x_buf[:, sl], pair).astype(BF16)
            down = dot_outer(c_buf[:, sl], hid[k]).astype(BF16)
            dpart[0, k, 0, sl, :] = both[:, :LANES]
            dpart[1, k, 0, sl, :] = both[:, LANES:CHUNK]
            dpart[0, k, 1, sl, :] = both[:, CHUNK : CHUNK + LANES]
            dpart[1, k, 1, sl, :] = both[:, CHUNK + LANES :]
            dpart[0, k, 2, sl, :] = down[:, :LANES]
            dpart[1, k, 2, sl, :] = down[:, LANES:]

        for m in range(3):
            remote(
                dpart.at[1 - c, k, m], dx_buf.at[k, m], one_sem.at[DS], dx_recv.at[3 * k + m], (d, mate)
            ).start()

    def rows_of(k, m, sl):
        return jnp.concatenate([w_buf[0, k, m, sl, :], w_buf[1, k, m, sl, :]], axis=1)

    def produce():
        @pl.loop(0, width // block)
        def _(i):
            sl = cols(i)
            acc = dot_rows(hid[0], rows_of(0, 2, sl))
            for k in range(1, chunks):
                acc += dot_rows(hid[k], rows_of(k, 2, sl))
            po[:, sl] = acc.astype(BF16)

    def pick_grads():
        @pl.loop(0, width // block)
        def _(i):
            sl = cols(i)
            acc = dot_rows(dgate[0], rows_of(0, 0, sl))
            acc += dot_rows(dup[0], rows_of(0, 1, sl))
            for k in range(1, chunks):
                acc += dot_rows(dgate[k], rows_of(k, 0, sl))
                acc += dot_rows(dup[k], rows_of(k, 1, sl))
            pg[:, sl] = acc.astype(BF16)

    def chain(km):
        k = lax.div(km, 3)
        m = lax.rem(km, 3)

        wait_bytes(dx_buf.at[k, m], dx_recv.at[km])

        @pl.loop(0, QUARTERS)
        def _(q):
            i = QUARTERS * km + q
            sl = pl.ds(pl.multiple_of(q * quarter, quarter), quarter)
            mine = piece(dpart.at[c], k, m, q)
            there = piece(ch_buf, k, m, q)
            own = dpart[c, k, m, sl, :].astype(F32) + dx_buf[k, m, sl, :].astype(F32)

            @pl.when(r == 1)
            def _():
                dpart[c, k, m, sl, :] = own.astype(BF16)

            @pl.when(r != 1)
            def _():
                wait_bytes(there, ch_recv.at[i])
                dpart[c, k, m, sl, :] = (own + ch_buf[k, m, sl, :].astype(F32)).astype(BF16)

            @pl.when(r != 0)
            def _():
                remote(mine, there, one_sem.at[HS], ch_recv.at[i], (d, nxt)).start()

        @pl.when(r == 0)
        def _():
            def share(t):
                return dpart.at[c, k, m, pl.ds(pl.multiple_of(t * depth, depth), depth)]

            @pl.when(native)
            def _():
                pltpu.make_async_copy(share(d), fg.at[c, k, m], one_sem.at[FL]).start()

            @pl.when(rootmate)
            def _():
                remote(share(d), fg.at[c, k, m], one_sem.at[FS], one_sem.at[FR], (d, d)).start()

            for t in others:
                remote(share(t), fg.at[c, k, m], one_sem.at[FS], one_sem.at[FR], (t, d)).start()

    @pl.loop(0, width // 512)
    def _(i):
        sl = cols(i, 512)
        st[:, sl] = dot(pick_a[...] + pick_b[...], tok_ref[:, sl]).astype(BF16)

    exchange(st, x_buf, TS, TR, TL)

    @pl.loop(0, width // 512)
    def _(i):
        sl = cols(i, 512)
        cot = cot_ref[:, sl].astype(F32)
        sc[:, sl] = (
            dot(pick_a[...], (gain_a * cot).astype(BF16))
            + dot(pick_b[...], (gain_b * cot).astype(BF16))
        ).astype(BF16)

    exchange(sc, c_buf, CS, CR, CL)

    middle = nz // 2
    early = r < middle
    late = jnp.logical_not(early)

    def groups(first, second, third):
        return jnp.where(r == 1, first, jnp.where(r == 2, second, jnp.where(r == 3, third, 0)))

    def sums(start, stop):
        @pl.loop(start, stop)
        def _(km):
            chain(km)

    @pl.loop(0, 6)
    def _(km):
        weights(km)

    @pl.when(early)
    def _():
        @pl.loop(6, 9)
        def _(km):
            weights(km)

    exchanged(x_buf, TR, TL)
    exchanged(c_buf, CR, CL)
    swapped(0)
    hidden_units(0)
    pl.when(late)(lambda: weights(6))
    outer(0)
    pl.when(late)(lambda: weights(7))
    swapped(1)
    hidden_units(1)
    pl.when(late)(lambda: weights(8))
    outer(1)
    sums(0, groups(3, 0, 0))
    swapped(2)
    hidden_units(2)
    sums(groups(3, 0, 0), groups(4, 0, 0))
    produce()
    exchange(po, bo, OS, OR, OL)
    sums(groups(4, 0, 0), groups(5, 2, 1))
    pick_grads()
    exchange(pg, bg, GS, GR, GL)
    sums(groups(5, 2, 1), groups(6, 3, 2))
    outer(2)
    def finish_rows():
        exchanged(bo, OR, OL)

        @pl.loop(0, width // 512)
        def _(i):
            sl = cols(i, 512)
            got = bo[:, sl]
            out_ref[:, sl] = (
                gain_a * dot_outer(pick_a[...], got) + gain_b * dot_outer(pick_b[...], got)
            ).astype(BF16)

        exchanged(bg, GR, GL)

        @pl.loop(0, width // 512)
        def _(i):
            sl = cols(i, 512)
            got = bg[:, sl]
            ingrad_ref[:, sl] = (
                dot_outer(pick_a[...], got) + dot_outer(pick_b[...], got)
            ).astype(BF16)

    last = jnp.logical_or(r == 0, r >= nz - 3)
    sums(groups(6, 3, 2), 8)
    pl.when(last)(finish_rows)
    sums(8, 9)
    pl.when(jnp.logical_not(last))(finish_rows)

    @pl.when(native)
    def _():
        wait_bytes(fg.at[0], one_sem.at[FL])
        wait_bytes(fg.at[0], one_sem.at[FR])
        wait_bytes(dpart.at[0, :, :, pl.ds(0, width - depth)], one_sem.at[FS])

    @pl.when(jnp.logical_not(native))
    def _():
        wait_bytes(fg, one_sem.at[FR])

    @pl.when(rootmate)
    def _():
        wait_bytes(dpart.at[0], one_sem.at[FS])

    for k in range(chunks):
        for h in range(2):
            sl = slice(CHUNK * k + LANES * h, CHUNK * k + LANES * (h + 1))
            gg_ref[0, :, sl] = fg[h, k, 0]
            gu_ref[0, :, sl] = fg[h, k, 1]
            gd_ref[0, :, sl] = fg[h, k, 2]

    for send, buf in ((TS, st), (CS, sc), (OS, po), (GS, pg)):
        wait_bytes(buf.at[pl.ds(0, rows - SLOTS)], one_sem.at[send])

    @pl.when(r <= nz - 2)
    def _():
        wait_bytes(w_buf.at[0], one_sem.at[WS])

    @pl.when(native)
    def _():
        wait_bytes(w_buf.at[0], one_sem.at[PS])

    @pl.when(jnp.logical_not(rootmate))
    def _():
        wait_bytes(w_buf.at[0], one_sem.at[XS])

    @pl.when(r != 0)
    def _():
        wait_bytes(ch_buf, one_sem.at[HS])

    wait_bytes(dx_buf, one_sem.at[DS])


def hand_over(*refs):
    for i in range(5):
        refs[5 + i][...] = refs[i][...]


def shards(n, tokens, routes, route_gains, cotangent, w_gate, w_up, w_down):
    width = tokens.shape[1]
    units = w_gate.shape[2]
    chunks = units // CHUNK
    count = tokens.shape[0]
    depth = width // n
    rows = n * SLOTS

    vmem = pl.BlockSpec(memory_space=pltpu.VMEM)
    anywhere = pl.BlockSpec(memory_space=pl.ANY)
    sem = pltpu.SemaphoreType.DMA
    share = jax.ShapeDtypeStruct((1, depth, units), BF16)
    row_out = jax.ShapeDtypeStruct((count, width), BF16)
    landed = pltpu.VMEM((rows, width), BF16)
    acts = pltpu.VMEM((chunks, rows, CHUNK), BF16)
    half = pltpu.VMEM((chunks, 3, width, LANES), BF16)
    halves = pltpu.VMEM((2, chunks, 3, width, LANES), BF16)
    results = pl.pallas_call(
        functools.partial(moe_kernel, n, n // 2),
        out_shape=(row_out, row_out, share, share, share),
        in_specs=[vmem] * 4 + [anywhere] * 3,
        out_specs=(vmem,) * 5,
        scratch_shapes=[
            pltpu.VMEM((rows, count), BF16),
            pltpu.VMEM((rows, count), BF16),
            halves,
            landed,
            landed,
            landed,
            landed,
            acts,
            acts,
            acts,
            halves,
            half,
            half,
            landed,
            landed,
            landed,
            landed,
            pltpu.VMEM((2, chunks, 3, depth, LANES), BF16),
            sem((3 * chunks,)),
            sem((3 * chunks * QUARTERS,)),
            sem((3 * chunks,)),
            sem((3 * chunks * QUARTERS,)),
            sem((3 * chunks,)),
            sem((20,)),
        ],
        compiler_params=pltpu.CompilerParams(
            collective_id=0, has_side_effects=True, vmem_limit_bytes=60 * 2**20
        ),
    )(routes.T, route_gains.T, tokens, cotangent, w_gate, w_up, w_down)
    return pl.pallas_call(
        hand_over,
        out_shape=(row_out, row_out, share, share, share),
        in_specs=[vmem] * 5,
        out_specs=(vmem,) * 5,
    )(*results)


def solution(mesh):
    rows = P(("dp", "expert"), None)
    weights = P("expert", None, None)
    shares = P("expert", "dp", None)
    return jax.shard_map(
        functools.partial(shards, mesh.shape["dp"]),
        mesh=mesh,
        in_specs=(rows, rows, rows, rows, weights, weights, weights),
        out_specs=(rows, rows, shares, shares, shares),
        check_vma=False,
    )
```

```python
import functools
import math

import jax
import jax.numpy as jnp
from jax import lax
from jax.experimental import pallas as pl
from jax.experimental.pallas import tpu as pltpu
from jax.sharding import PartitionSpec as P

SLOTS = 32
LANES = 128
CHUNK = 256
QUARTERS = 8
MESH = pl.DeviceIdType.MESH
OFFSETS = (
    (1, 0), (3, 0), (0, 1), (0, 3), (1, 1), (3, 3), (1, 3), (3, 1),
    (2, 0), (0, 2), (2, 2), (2, 1), (1, 2), (2, 3), (3, 2),
)
F32 = jnp.float32
BF16 = jnp.bfloat16


def dot(a, b):
    return jnp.dot(a, b, preferred_element_type=F32)


def dot_rows(a, b):
    return lax.dot_general(a, b, (((1,), (1,)), ((), ())), preferred_element_type=F32)


def dot_outer(a, b):
    return lax.dot_general(a, b, (((0,), (0,)), ((), ())), preferred_element_type=F32)


def moe_kernel(
    n,
    nz,
    routes_ref,
    gains_ref,
    tok_ref,
    cot_ref,
    wg_ref,
    wu_ref,
    wd_ref,
    out_ref,
    ingrad_ref,
    gg_ref,
    gu_ref,
    gd_ref,
    pick_a,
    pick_b,
    w_buf,
    st,
    sc,
    x_buf,
    c_buf,
    hid,
    dgate,
    dup,
    dpart,
    dx_buf,
    ch_buf,
    po,
    pg,
    bo,
    bg,
    fg,
    loc_sem,
    w_recv,
    x_recv,
    ch_recv,
    dx_recv,
    one_sem,
):
    (TS, TR, TL, CS, CR, CL, OS, OR, OL, GS, GR, GL, WS, PS, XS, HS, DS, FS, FR, FL) = range(20)
    width = tok_ref.shape[1]
    chunks = w_buf.shape[1]
    rows = n * SLOTS
    quarter = width // QUARTERS
    depth = width // n
    block = 256
    row_block = min(block, rows)

    d = lax.axis_index("dp")
    ex = lax.axis_index("expert")
    z = lax.div(ex, 2)
    c = lax.rem(ex, 2)
    sgn = 1 - 2 * c
    r = lax.rem(sgn * (z - lax.div(d, 2)) + nz, nz)
    nxt = 2 * lax.rem(z + sgn + nz, nz) + c
    prv = 2 * lax.rem(z - sgn + nz, nz) + c
    mate = ex + sgn
    native = ex == d
    rootmate = mate == d
    side = math.isqrt(n)
    others = [
        lax.rem(lax.div(d, side) + a, side) * side + lax.rem(lax.rem(d, side) + b, side)
        for a, b in OFFSETS
        if a < side and b < side
    ]

    def remote(src, dst, send, recv, dev):
        return pltpu.make_async_remote_copy(
            src_ref=src, dst_ref=dst, send_sem=send, recv_sem=recv, device_id=dev, device_id_type=MESH
        )

    def wait_bytes(ref, sem):
        pltpu.make_async_copy(ref, ref, sem).wait()

    barrier = pltpu.get_barrier_semaphore()

    def greet(dev):
        pl.semaphore_signal(barrier, inc=1, device_id=dev, device_id_type=MESH)

    @pl.loop(1, n)
    def _(j):
        greet((lax.rem(d + j, n), ex))

    greet((d, mate))
    greet((d, nxt))
    greet((d, prv))

    @pl.when(d != ex)
    def _():
        greet((ex, mate))

    @pl.when(rootmate)
    def _():
        @pl.loop(1, n)
        def _(j):
            greet((lax.rem(d + j, n), d))

    @pl.when(native)
    def _():
        for k in range(chunks):
            for m, ref in enumerate((wg_ref, wu_ref, wd_ref)):
                for h in range(2):
                    pltpu.make_async_copy(
                        ref.at[0, :, pl.ds(CHUNK * k + LANES * h, LANES)],
                        w_buf.at[h, k, m],
                        loc_sem.at[3 * k + m],
                    ).start()

    count = tok_ref.shape[0]

    def iota(shape, dim):
        return lax.broadcasted_iota(jnp.int32, shape, dim)

    def ones(mask):
        return jnp.where(mask, 1.0, 0.0).astype(BF16)

    names = [routes_ref[k : k + 1, :] for k in range(2)]
    named = [name == iota((n, count), 0) for name in names]
    square = (count, count)
    before = dot(ones(named[0]) + ones(named[1]), ones(iota(square, 0) < iota(square, 1)))
    for buf, name, match in zip((pick_a, pick_b), names, named):
        place = jnp.sum(jnp.where(match, before, 0.0), axis=0, keepdims=True).astype(jnp.int32)
        buf[...] = ones(iota((rows, count), 0) == name * SLOTS + place)
    gain_a, gain_b = [
        jnp.sum(
            jnp.where(iota(square, 0) == iota(square, 1), gains_ref[k : k + 1, :], 0.0),
            axis=1,
            keepdims=True,
        )
        for k in range(2)
    ]

    pl.semaphore_wait(
        barrier, n + 2 + jnp.where(d != ex, 1, 0) + jnp.where(rootmate, n - 1, 0)
    )

    def slot_rows(i):
        return pl.ds(pl.multiple_of(i * SLOTS, SLOTS), SLOTS)

    def exchange(src, dst, send, recv, own):
        pltpu.make_async_copy(src.at[slot_rows(d)], dst.at[slot_rows(d)], one_sem.at[own]).start()

        for t in others:
            remote(
                src.at[slot_rows(t)], dst.at[slot_rows(d)], one_sem.at[send], one_sem.at[recv], (t, ex)
            ).start()

    def exchanged(dst, recv, own):
        wait_bytes(dst.at[pl.ds(0, SLOTS)], one_sem.at[own])
        wait_bytes(dst.at[pl.ds(0, rows - SLOTS)], one_sem.at[recv])

    def cols(i, size=block):
        return pl.ds(pl.multiple_of(i * size, size), size)

    def piece(buf, k, m, q):
        return buf.at[k, m, pl.ds(pl.multiple_of(q * quarter, quarter), quarter)]

    def weights(km):
        k = lax.div(km, 3)
        m = lax.rem(km, 3)

        @pl.when(native)
        def _():
            wait_bytes(w_buf.at[:, k, m], loc_sem.at[km])

        @pl.loop(0, QUARTERS)
        def _(q):
            i = QUARTERS * km + q
            mine = piece(w_buf.at[c], k, m, q)

            @pl.when(jnp.logical_not(native))
            def _():
                wait_bytes(mine, w_recv.at[i])

            @pl.when(r <= nz - 2)
            def _():
                remote(mine, mine, one_sem.at[WS], w_recv.at[i], (d, nxt)).start()

            @pl.when(native)
            def _():
                other = piece(w_buf.at[1 - c], k, m, q)
                remote(other, other, one_sem.at[PS], w_recv.at[i], (d, mate)).start()

        @pl.when(jnp.logical_not(rootmate))
        def _():
            half = w_buf.at[c, k, m]
            remote(half, half, one_sem.at[XS], x_recv.at[km], (d, mate)).start()

    def swapped(k):
        @pl.when(jnp.logical_not(native))
        def _():
            @pl.loop(0, 3)
            def _(m):
                wait_bytes(w_buf.at[1 - c, k, m], x_recv.at[3 * k + m])

    def mat(k, m):
        return jnp.concatenate([w_buf[0, k, m], w_buf[1, k, m]], axis=1)

    def hidden_units(k):
        @pl.loop(0, rows // row_block)
        def _(i):
            sl = cols(i, row_block)
            x = x_buf[sl, :]
            gate = dot(x, mat(k, 0))
            up = dot(x, mat(k, 1))
            sigma = jax.nn.sigmoid(gate)
            act = gate * sigma
            hid[k, sl, :] = (act * up).astype(BF16)
            dh = dot(c_buf[sl, :], mat(k, 2))
            dgate[k, sl, :] = (dh * up * (sigma * (1.0 + gate * (1.0 - sigma)))).astype(BF16)
            dup[k, sl, :] = (dh * act).astype(BF16)

    def outer(k):
        @pl.loop(0, width // block)
        def _(i):
            sl = cols(i)
            pair = jnp.concatenate([dgate[k], dup[k]], axis=1)
            both = dot_outer(x_buf[:, sl], pair).astype(BF16)
            down = dot_outer(c_buf[:, sl], hid[k]).astype(BF16)
            dpart[0, k, 0, sl, :] = both[:, :LANES]
            dpart[1, k, 0, sl, :] = both[:, LANES:CHUNK]
            dpart[0, k, 1, sl, :] = both[:, CHUNK : CHUNK + LANES]
            dpart[1, k, 1, sl, :] = both[:, CHUNK + LANES :]
            dpart[0, k, 2, sl, :] = down[:, :LANES]
            dpart[1, k, 2, sl, :] = down[:, LANES:]

        for m in range(3):
            remote(
                dpart.at[1 - c, k, m], dx_buf.at[k, m], one_sem.at[DS], dx_recv.at[3 * k + m], (d, mate)
            ).start()

    def rows_of(k, m, sl):
        return jnp.concatenate([w_buf[0, k, m, sl, :], w_buf[1, k, m, sl, :]], axis=1)

    def produce():
        @pl.loop(0, width // block)
        def _(i):
            sl = cols(i)
            acc = dot_rows(hid[0], rows_of(0, 2, sl))
            for k in range(1, chunks):
                acc += dot_rows(hid[k], rows_of(k, 2, sl))
            po[:, sl] = acc.astype(BF16)

    def pick_grads():
        @pl.loop(0, width // block)
        def _(i):
            sl = cols(i)
            acc = dot_rows(dgate[0], rows_of(0, 0, sl))
            acc += dot_rows(dup[0], rows_of(0, 1, sl))
            for k in range(1, chunks):
                acc += dot_rows(dgate[k], rows_of(k, 0, sl))
                acc += dot_rows(dup[k], rows_of(k, 1, sl))
            pg[:, sl] = acc.astype(BF16)

    def chain(km):
        k = lax.div(km, 3)
        m = lax.rem(km, 3)

        wait_bytes(dx_buf.at[k, m], dx_recv.at[km])

        @pl.loop(0, QUARTERS)
        def _(q):
            i = QUARTERS * km + q
            sl = pl.ds(pl.multiple_of(q * quarter, quarter), quarter)
            mine = piece(dpart.at[c], k, m, q)
            there = piece(ch_buf, k, m, q)
            own = dpart[c, k, m, sl, :].astype(F32) + dx_buf[k, m, sl, :].astype(F32)

            @pl.when(r == 1)
            def _():
                dpart[c, k, m, sl, :] = own.astype(BF16)

            @pl.when(r != 1)
            def _():
                wait_bytes(there, ch_recv.at[i])
                dpart[c, k, m, sl, :] = (own + ch_buf[k, m, sl, :].astype(F32)).astype(BF16)

            @pl.when(r != 0)
            def _():
                remote(mine, there, one_sem.at[HS], ch_recv.at[i], (d, nxt)).start()

        @pl.when(r == 0)
        def _():
            def share(t):
                return dpart.at[c, k, m, pl.ds(pl.multiple_of(t * depth, depth), depth)]

            @pl.when(native)
            def _():
                pltpu.make_async_copy(share(d), fg.at[c, k, m], one_sem.at[FL]).start()

            @pl.when(rootmate)
            def _():
                remote(share(d), fg.at[c, k, m], one_sem.at[FS], one_sem.at[FR], (d, d)).start()

            for t in others:
                remote(share(t), fg.at[c, k, m], one_sem.at[FS], one_sem.at[FR], (t, d)).start()

    pl.when(native)(lambda: weights(0))

    @pl.loop(0, width // 512)
    def _(i):
        sl = cols(i, 512)
        st[:, sl] = dot(pick_a[...] + pick_b[...], tok_ref[:, sl]).astype(BF16)

    exchange(st, x_buf, TS, TR, TL)
    pl.when(native)(lambda: weights(1))

    @pl.loop(0, width // 512)
    def _(i):
        sl = cols(i, 512)
        cot = cot_ref[:, sl].astype(F32)
        sc[:, sl] = (
            dot(pick_a[...], (gain_a * cot).astype(BF16))
            + dot(pick_b[...], (gain_b * cot).astype(BF16))
        ).astype(BF16)

    exchange(sc, c_buf, CS, CR, CL)

    middle = nz // 2
    early = r < middle
    late = jnp.logical_not(early)

    def groups(first, second, third):
        return jnp.where(r == 1, first, jnp.where(r == 2, second, jnp.where(r == 3, third, 0)))

    def sums(start, stop):
        @pl.loop(start, stop)
        def _(km):
            chain(km)

    @pl.loop(jnp.where(native, 2, 0), 6)
    def _(km):
        weights(km)

    @pl.when(early)
    def _():
        @pl.loop(6, 9)
        def _(km):
            weights(km)

    exchanged(x_buf, TR, TL)
    exchanged(c_buf, CR, CL)
    swapped(0)
    hidden_units(0)
    pl.when(late)(lambda: weights(6))
    outer(0)
    pl.when(late)(lambda: weights(7))
    swapped(1)
    hidden_units(1)
    pl.when(late)(lambda: weights(8))
    outer(1)
    sums(0, groups(3, 0, 0))
    swapped(2)
    hidden_units(2)
    sums(groups(3, 0, 0), groups(4, 0, 0))
    produce()
    exchange(po, bo, OS, OR, OL)
    sums(groups(4, 0, 0), groups(5, 2, 1))
    pick_grads()
    exchange(pg, bg, GS, GR, GL)
    sums(groups(5, 2, 1), groups(6, 3, 2))
    outer(2)
    def finish_rows():
        exchanged(bo, OR, OL)

        @pl.loop(0, width // 512)
        def _(i):
            sl = cols(i, 512)
            got = bo[:, sl]
            out_ref[:, sl] = (
                gain_a * dot_outer(pick_a[...], got) + gain_b * dot_outer(pick_b[...], got)
            ).astype(BF16)

        exchanged(bg, GR, GL)

        @pl.loop(0, width // 512)
        def _(i):
            sl = cols(i, 512)
            got = bg[:, sl]
            ingrad_ref[:, sl] = (
                dot_outer(pick_a[...], got) + dot_outer(pick_b[...], got)
            ).astype(BF16)

    last = jnp.logical_or(r == 0, r >= nz - 3)
    sums(groups(6, 3, 2), 8)
    pl.when(last)(finish_rows)
    sums(8, 9)
    pl.when(jnp.logical_not(last))(finish_rows)

    @pl.when(native)
    def _():
        wait_bytes(fg.at[0], one_sem.at[FL])
        wait_bytes(fg.at[0], one_sem.at[FR])
        wait_bytes(dpart.at[0, :, :, pl.ds(0, width - depth)], one_sem.at[FS])

    @pl.when(jnp.logical_not(native))
    def _():
        wait_bytes(fg, one_sem.at[FR])

    @pl.when(rootmate)
    def _():
        wait_bytes(dpart.at[0], one_sem.at[FS])

    for k in range(chunks):
        for h in range(2):
            sl = slice(CHUNK * k + LANES * h, CHUNK * k + LANES * (h + 1))
            gg_ref[0, :, sl] = fg[h, k, 0]
            gu_ref[0, :, sl] = fg[h, k, 1]
            gd_ref[0, :, sl] = fg[h, k, 2]

    for send, buf in ((TS, st), (CS, sc), (OS, po), (GS, pg)):
        wait_bytes(buf.at[pl.ds(0, rows - SLOTS)], one_sem.at[send])

    @pl.when(r <= nz - 2)
    def _():
        wait_bytes(w_buf.at[0], one_sem.at[WS])

    @pl.when(native)
    def _():
        wait_bytes(w_buf.at[0], one_sem.at[PS])

    @pl.when(jnp.logical_not(rootmate))
    def _():
        wait_bytes(w_buf.at[0], one_sem.at[XS])

    @pl.when(r != 0)
    def _():
        wait_bytes(ch_buf, one_sem.at[HS])

    wait_bytes(dx_buf, one_sem.at[DS])


def hand_over(*refs):
    for i in range(5):
        refs[5 + i][...] = refs[i][...]


def shards(n, tokens, routes, route_gains, cotangent, w_gate, w_up, w_down):
    width = tokens.shape[1]
    units = w_gate.shape[2]
    chunks = units // CHUNK
    count = tokens.shape[0]
    depth = width // n
    rows = n * SLOTS

    vmem = pl.BlockSpec(memory_space=pltpu.VMEM)
    anywhere = pl.BlockSpec(memory_space=pl.ANY)
    sem = pltpu.SemaphoreType.DMA
    share = jax.ShapeDtypeStruct((1, depth, units), BF16)
    row_out = jax.ShapeDtypeStruct((count, width), BF16)
    landed = pltpu.VMEM((rows, width), BF16)
    acts = pltpu.VMEM((chunks, rows, CHUNK), BF16)
    half = pltpu.VMEM((chunks, 3, width, LANES), BF16)
    halves = pltpu.VMEM((2, chunks, 3, width, LANES), BF16)
    results = pl.pallas_call(
        functools.partial(moe_kernel, n, n // 2),
        out_shape=(row_out, row_out, share, share, share),
        in_specs=[vmem] * 4 + [anywhere] * 3,
        out_specs=(vmem,) * 5,
        scratch_shapes=[
            pltpu.VMEM((rows, count), BF16),
            pltpu.VMEM((rows, count), BF16),
            halves,
            landed,
            landed,
            landed,
            landed,
            acts,
            acts,
            acts,
            halves,
            half,
            half,
            landed,
            landed,
            landed,
            landed,
            pltpu.VMEM((2, chunks, 3, depth, LANES), BF16),
            sem((3 * chunks,)),
            sem((3 * chunks * QUARTERS,)),
            sem((3 * chunks,)),
            sem((3 * chunks * QUARTERS,)),
            sem((3 * chunks,)),
            sem((20,)),
        ],
        compiler_params=pltpu.CompilerParams(
            collective_id=0, has_side_effects=True, vmem_limit_bytes=60 * 2**20
        ),
    )(routes.T, route_gains.T, tokens, cotangent, w_gate, w_up, w_down)
    return pl.pallas_call(
        hand_over,
        out_shape=(row_out, row_out, share, share, share),
        in_specs=[vmem] * 5,
        out_specs=(vmem,) * 5,
    )(*results)


def solution(mesh):
    rows = P(("dp", "expert"), None)
    weights = P("expert", None, None)
    shares = P("expert", "dp", None)
    return jax.shard_map(
        functools.partial(shards, mesh.shape["dp"]),
        mesh=mesh,
        in_specs=(rows, rows, rows, rows, weights, weights, weights),
        out_specs=(rows, rows, shares, shares, shares),
        check_vma=False,
    )
```
